512 devices in a mesh: blk: 128 (over x, z_hi, y, core), sub: 4 (over z_lo).
Axes of the slice: x: 4, y: 8, z: 8 (z_hi: 2, z_lo: 4; z = z_hi * 4 + z_lo), core: 2. Of those that a mesh axis runs over, the one named last changes fastest.
Arguments:
- images: bfloat16 [16384, 1152], P(('blk', 'sub')), may hold values from -0.19921875 to 0.19921875
- texts: bfloat16 [16384, 1152], P(('blk', 'sub')), may hold values from -0.19921875 to 0.19921875
- row_counts: int32 [128], replicated, may hold values from 32 to 128, as said below
- log_temp: float32 [1], replicated, may hold values from 3 to 4.1
- bias: float32 [1], replicated, may hold values from -10 to -6
Outputs:
- loss: float32 [1], replicated
- grad_log_temp: float32 [1], replicated
- grad_bias: float32 [1], replicated
- grad_images: float32 [16384, 1152], P(('blk', 'sub'))
- grad_texts: float32 [16384, 1152], P(('blk', 'sub'))
The draws below stay inside these ranges and needn't reach their ends.
Inputs may be any that keep to these rules, and one draw needn't show every extreme that they name: `row_counts`: each count is a multiple of 32; some member holds exactly 128.
All inputs are finite; a program needn't handle non-finite values.
Results may differ from the reference program's by a relative error of at most 0.0035.
The reference program's roundings to bfloat16 on the way (of `weight`) count: a program that leaves them out, or rounds other values in their place, can miss the bound.
Values may be sent and summed in bfloat16 or wider, within the bound.
A program may use at most 64 MiB of HBM per device.

```python
import jax
import jax.numpy as jnp
from jax import lax

D = 1152
CAP = 128
QUART = 32
ROWS = 16384
N_BLK = 128
N_SUB = 4


def draw_row_counts(key, part):
    key = jax.random.fold_in(key, 7)
    first, second, third = jax.random.split(key, 3)
    left = jax.random.randint(first, (N_BLK,), 0, 4)
    right = jax.random.randint(second, (N_BLK,), 0, 4)
    tiles = jnp.minimum(1 + left * right // 3, N_SUB)
    heavy = jax.random.randint(third, (), 0, N_BLK)
    tiles = tiles.at[heavy].set(N_SUB)
    return (tiles * QUART).astype(jnp.int32)


def steps_of(own_key, shape, cuts, low, top_value):
    gain, own = 1.0, jax.random.fold_in(own_key, 6)
    for position, blocks in cuts:
        draws = jnp.exp(jax.random.uniform(jax.random.fold_in(own, position), (blocks,), jnp.float32, low / len(cuts), top_value / len(cuts)))
        gain = gain * jnp.repeat(draws, shape[position] // blocks).reshape([-1 if axis == position else 1 for axis in range(len(shape))])
    return gain


def bell_draw(rng, dims, scale, most, shards=(), kind=jnp.bfloat16):
    array = scale * jax.random.normal(rng, dims, jnp.float32)
    if shards:
        array = array * steps_of(rng, dims, shards, -0.22, 0.18)
    return jnp.clip(array, -most, most).astype(kind)


def setup_inputs(seed: int = 0) -> dict:
    key_of = jax.random.split(jax.random.key(seed), 6)
    return {
        "images": bell_draw(key_of[0], (ROWS, D), 0.03, 0.19921875, ((0, 512),)),
        "texts": bell_draw(key_of[1], (ROWS, D), 0.03, 0.19921875, ((0, 512),)),
        "row_counts": draw_row_counts(jax.random.fold_in(key_of[5], 71), 0),
        "log_temp": jnp.clip(jax.random.uniform(key_of[3], (1,), jnp.float32, 3.0, 4.1), 3.0, 4.1),
        "bias": jnp.clip(jax.random.uniform(key_of[4], (1,), jnp.float32, -10.0, -6.0), -10.0, -6.0),
    }


def normalize(values):
    wide = values.astype(jnp.float32)
    length = jnp.sqrt(lax.optimization_barrier(jnp.sum(wide * wide, axis=1, keepdims=True)) + 1e-06)
    return (wide / length, length)

def project(grad, unit, length):
    return (grad - unit * lax.optimization_barrier(jnp.sum(unit * grad, axis=1, keepdims=True))) / length

def reference(images, texts, row_counts, log_temp, bias):
    temp = jnp.exp(log_temp[0])
    shift = bias[0]
    img_unit, img_length = normalize(images)
    txt_unit, txt_length = normalize(texts)
    img_half = img_unit.astype(jnp.bfloat16)
    txt_half = txt_unit.astype(jnp.bfloat16)
    slots = jnp.arange(CAP, dtype=jnp.int32)
    used_mask = slots[None, :] < row_counts[:, None]
    txt_used = used_mask.reshape(-1)
    columns = jnp.arange(N_BLK * CAP, dtype=jnp.int32)
    used = jnp.sum(row_counts).astype(jnp.float32)
    blocks = img_half.reshape(N_BLK, CAP, D)
    members = jnp.arange(N_BLK, dtype=jnp.int32)

    def visit(carry, inputs):
        txt_dir, sums = carry
        member, block, live = inputs
        logits = temp * lax.dot_general(block, txt_half, (((1,), (1,)), ((), ())), preferred_element_type=jnp.float32) + shift
        own = member * CAP + slots
        sign = jnp.where(own[:, None] == columns[None, :], 1.0, -1.0)
        mask = live[:, None] & txt_used[None, :]
        pair = jnp.where(mask, jax.nn.softplus(-sign * logits), 0.0)
        slope = jnp.where(mask, -sign * jax.nn.sigmoid(-sign * logits), 0.0)
        weight = (slope * temp).astype(jnp.bfloat16)
        img_dir = jnp.dot(weight, txt_half, preferred_element_type=jnp.float32)
        txt_dir = txt_dir + lax.dot_general(weight, block, (((0,), (0,)), ((), ())), preferred_element_type=jnp.float32)
        sums = sums + jnp.stack([jnp.sum(pair), jnp.sum(slope), jnp.sum(slope * (logits - shift))])
        return ((txt_dir, sums), img_dir)
    start = (jnp.zeros((N_BLK * CAP, D), jnp.float32), jnp.zeros((3,), jnp.float32))
    (txt_dir, sums), img_dirs = lax.scan(visit, start, (members, blocks, used_mask))
    img_dir = img_dirs.reshape(N_BLK * CAP, D)
    loss = sums[0:1] / used
    grad_log_temp = sums[2:3] / used
    grad_bias = sums[1:2] / used
    grad_images = project(img_dir, img_unit, img_length)
    grad_texts = project(txt_dir, txt_unit, txt_length)
    return (loss, grad_log_temp, grad_bias, grad_images, grad_texts)
```

```python
import functools

import jax
import jax.numpy as jnp
from jax import lax
from jax.experimental import pallas as pl
from jax.experimental.pallas import tpu as pltpu
from jax.sharding import PartitionSpec as P

MESH = pl.DeviceIdType.MESH
F32 = jnp.float32
BF16 = jnp.bfloat16
T = 32
RING = 8
NEAR_FIRST = (1, 7, 2, 6, 3, 5, 4)

IMG, TXT, RED_C, RED_XT, RED_Z, RED_XI, RED_Y, SCAL = 0, 16, 48, 64, 72, 80, 88, 96
N_SEM = 120


def place():
    blk, sub = lax.axis_index("blk"), lax.axis_index("sub")
    core = lax.rem(blk, 2)
    y = lax.rem(lax.div(blk, 2), RING)
    z = lax.rem(lax.div(blk, 16), 2) * 4 + sub
    x = lax.div(blk, 32)
    return x, y, z, core


def member(x, y, z, core):
    return ((x * 2 + lax.div(z, 4)) * RING + y) * 2 + core


def device(x, y, z, core):
    return (member(x, y, z, core), lax.rem(z, 4))


def ring(value):
    return lax.rem(value, RING)


def normalized(values):
    wide = values.astype(F32)
    length = jnp.sqrt(jnp.sum(wide * wide, axis=1, keepdims=True) + 1e-06)
    return wide / length, length


def projected(grad, unit, length):
    return (grad - unit * jnp.sum(unit * grad, axis=1, keepdims=True)) / length


def sigmoid_and_softplus(u):
    small = jnp.exp(-jnp.abs(u))
    ratio = 1.0 / (1.0 + small)
    sigmoid = jnp.where(u >= 0.0, ratio, small * ratio)
    softplus = jnp.maximum(u, 0.0) + jnp.log1p(small)
    return sigmoid, softplus


def tile(slot):
    return pl.ds(slot * T, T)


def kernel(
    img_in, txt_in, counts, counts_row, log_temp, bias,
    loss, grad_log_temp, grad_bias, grad_img, grad_txt,
    img, txt, weight, logits, txt_part, img_part, part_a, part_b, part_i,
    from_c, from_xt, from_z, from_xi, from_y, scal, ssem, rsem,
):
    x, y, z, core = place()
    pair_i = x + 1 - 2 * lax.rem(x, 2)
    pair_t = lax.rem(x + 3 + 2 * lax.rem(x, 2), 4)

    def y_peer(d):
        return device(x, ring(y + d), z, core)

    def z_peer(d):
        return device(x, y, ring(z + d), core)

    my_xc = x * 2 + core

    def xc_peer(d):
        other = ring(my_xc + d)
        return device(lax.div(other, 2), y, z, lax.rem(other, 2))

    img_mate = device(pair_i, y, z, core)
    txt_mate = device(pair_t, y, z, core)
    core_mate = device(x, y, z, 1 - core)

    barrier = pltpu.get_barrier_semaphore()
    for d in range(1, RING):
        for peer in (y_peer(d), z_peer(d), xc_peer(d)):
            pl.semaphore_signal(barrier, inc=1, device_id=peer, device_id_type=MESH)

    temp = jnp.exp(jnp.full((1, 1), log_temp[0], F32))
    shift = bias[0]
    img_unit, img_length = normalized(img_in[...])
    txt_unit, txt_length = normalized(txt_in[...])

    def tile_used(x, y, z, core):
        return jnp.where(counts[member(x, y, z, core)] > T * lax.rem(z, 4), 1.0, 0.0)

    own_used = tile_used(x, y, z, core)
    img_half = jnp.where(own_used > 0.0, img_unit, 0.0).astype(BF16)
    txt_half = jnp.where(own_used > 0.0, txt_unit, 0.0).astype(BF16)
    img[tile(0), :] = img_half
    txt[tile(0), :] = txt_half

    def copy(src, dst, index, peer):
        return pltpu.make_async_remote_copy(
            src_ref=src,
            dst_ref=dst,
            send_sem=ssem.at[index],
            recv_sem=rsem.at[index],
            device_id=peer,
            device_id_type=MESH,
        )

    sent = []

    def start(made):
        made.start()
        sent.append(made)
        return made

    pl.semaphore_wait(barrier, 3 * (RING - 1))

    img_got, txt_got = {}, {}
    for s in NEAR_FIRST:
        txt_got[s] = start(copy(txt.at[tile(0)], txt.at[tile(s)], TXT + s, z_peer(RING - s)))
        img_got[s] = start(copy(img.at[tile(0)], img.at[tile(s)], IMG + s, y_peer(RING - s)))

    def pass_on(s):
        txt_got[8 + s] = start(copy(txt.at[tile(s)], txt.at[tile(8 + s)], TXT + 8 + s, txt_mate))
        img_got[8 + s] = start(copy(img.at[tile(s)], img.at[tile(8 + s)], IMG + 8 + s, img_mate))
        txt_got[16 + s] = start(copy(txt.at[tile(s)], txt.at[tile(16 + s)], TXT + 16 + s, core_mate))

    pass_on(0)

    img_wide, txt_wide = img_half.astype(F32), txt_half.astype(F32)
    own_u = temp * jnp.sum(img_wide * txt_wide, axis=1, keepdims=True) + shift
    own_sigmoid, own_softplus = sigmoid_and_softplus(-own_u)
    own_slope = -own_sigmoid * own_used
    own_pair = own_softplus * own_used
    own_weight = (own_slope * temp).astype(BF16).astype(F32)
    own_sums = (jnp.sum(own_pair), jnp.sum(own_slope), jnp.sum(own_slope * (own_u - shift)))

    for s in NEAR_FIRST:
        txt_got[s].wait_recv()
        img_got[s].wait_recv()
        pass_on(s)
    for s in (0, *NEAR_FIRST):
        txt_got[8 + s].wait_recv()
        txt_got[24 + s] = start(copy(txt.at[tile(8 + s)], txt.at[tile(24 + s)], TXT + 24 + s, core_mate))
    for s in (0, *NEAR_FIRST):
        img_got[8 + s].wait_recv()
        txt_got[16 + s].wait_recv()
        txt_got[24 + s].wait_recv()

    def block(c, sums):
        rows = pl.ds(pl.multiple_of(c * 256, 256), 256)
        logits[...] = lax.dot_general(
            txt[rows, :], img[...], (((1,), (1,)), ((), ())), preferred_element_type=F32
        )
        tx = jnp.where(lax.rem(c, 2) == 1, pair_t, x)
        tc = jnp.where(c >= 2, 1 - core, core)
        pair_sum, slope_sum, scaled_sum = sums
        for k in range(8):
            scaled = logits[tile(k), :] * temp
            u = scaled + shift
            slope, pair = sigmoid_and_softplus(u)
            if k == 0:
                row = lax.broadcasted_iota(jnp.int32, (T, 512), 0)
                column = lax.broadcasted_iota(jnp.int32, (T, 512), 1)
                own = (row == column) & (c == 0)
                slope = jnp.where(own, 0.0, slope)
                pair = jnp.where(own, 0.0, pair)
            weight[pl.ds(pl.multiple_of(c * 256 + k * T, T), T), :] = (slope * temp).astype(BF16)
            used = tile_used(tx, y, ring(z + k), tc)

            def folded(value):
                return jnp.sum(value.reshape(T // 8, 8, 512), axis=0)

            pair_sum = pair_sum + used * folded(pair)
            slope_sum = slope_sum + used * folded(slope)
            scaled_sum = scaled_sum + folded(slope * scaled)
        return pair_sum, slope_sum, scaled_sum

    zero = jnp.zeros((8, 512), F32)
    pair_sum, slope_sum, scaled_sum = lax.fori_loop(0, 4, block, (zero, zero, zero))

    column_tile = lax.broadcasted_iota(jnp.int32, (8, 512), 1) // T
    columns_used = zero
    for s in range(16):
        used = tile_used(x if s < 8 else pair_i, ring(y + s), z, core)
        columns_used = jnp.where(column_tile == s, used, columns_used)
    sums = (
        jnp.sum(pair_sum * columns_used) + own_sums[0],
        jnp.sum(slope_sum * columns_used) + own_sums[1],
        jnp.sum(scaled_sum) + own_sums[2],
    )
    lane = lax.broadcasted_iota(jnp.int32, (8, 128), 1)
    vector = jnp.where(lane == 0, sums[0], jnp.where(lane == 1, sums[1], jnp.where(lane == 2, sums[2], 0.0)))

    def spread(stage, mine, peer_of, value):
        scal[stage, mine] = value
        for d in range(1, RING):
            index = SCAL + stage * 8 + mine
            made = pltpu.make_async_remote_copy(
                src_ref=scal.at[stage, mine],
                dst_ref=scal.at[stage, mine],
                send_sem=ssem.at[SCAL + stage * 8 + d],
                recv_sem=rsem.at[index],
                device_id=peer_of(d),
                device_id_type=MESH,
            )
            start(made)

    def summed(stage, mine, peer_of):
        for d in range(1, RING):
            other = ring(mine + d)
            pltpu.make_async_remote_copy(
                src_ref=scal.at[stage, mine],
                dst_ref=scal.at[stage, other],
                send_sem=ssem.at[SCAL + stage * 8 + d],
                recv_sem=rsem.at[SCAL + stage * 8 + other],
                device_id=peer_of(d),
                device_id_type=MESH,
            ).wait_recv()
        total = scal[stage, 0]
        for k in range(1, RING):
            total = total + scal[stage, k]
        return total

    spread(0, y, y_peer, vector)

    def image_dir(first):
        return lax.dot_general(
            weight[:, first : first + 256], txt[...], (((0,), (0,)), ((), ())), preferred_element_type=F32
        )

    def text_dir(first):
        return jnp.dot(weight[first : first + 256, :], img[...], preferred_element_type=F32)

    img_part[256:512, :] = image_dir(256).astype(BF16)
    xi = {}
    for s in range(8):
        xi[s] = start(copy(img_part.at[tile(8 + s)], from_xi.at[tile(s)], RED_XI + s, img_mate))

    txt_part[768:1024, :] = text_dir(768).astype(BF16)
    c_d = start(copy(txt_part.at[pl.ds(768, 256)], from_c.at[pl.ds(256, 256)], RED_C + 1, core_mate))
    part_b[...] = text_dir(256)

    total = summed(0, y, y_peer)
    spread(1, z, z_peer, total)

    c_d.wait_recv()
    xt = {}
    for s in range(8):
        both = part_b[tile(s), :] + from_c[tile(8 + s), :].astype(F32)
        txt_part[tile(8 + s), :] = both.astype(BF16)
        xt[s] = start(copy(txt_part.at[tile(8 + s)], from_xt.at[tile(s)], RED_XT + s, txt_mate))

    txt_part[512:768, :] = text_dir(512).astype(BF16)
    c_c = start(copy(txt_part.at[pl.ds(512, 256)], from_c.at[pl.ds(0, 256)], RED_C, core_mate))
    part_i[...] = image_dir(0)
    part_a[...] = text_dir(0)

    total = summed(1, z, z_peer)
    spread(2, my_xc, xc_peer, total)

    got_y, got_z = {}, {}
    c_c.wait_recv()
    order = (4, 3, 5, 2, 6, 1, 7, 0)
    for s in order:
        xi[s].wait_recv()
        both = part_i[tile(s), :] + from_xi[tile(s), :].astype(F32)
        if s == 0:
            img_dir = both
        else:
            img_part[tile(s), :] = both.astype(BF16)
            got_y[RING - s] = start(copy(img_part.at[tile(s)], from_y.at[tile(RING - s)], RED_Y + RING - s, y_peer(s)))
        xt[s].wait_recv()
        both = part_a[tile(s), :] + from_c[tile(s), :].astype(F32) + from_xt[tile(s), :].astype(F32)
        if s == 0:
            txt_dir = both
        else:
            txt_part[tile(s), :] = both.astype(BF16)
            got_z[RING - s] = start(copy(txt_part.at[tile(s)], from_z.at[tile(RING - s)], RED_Z + RING - s, z_peer(s)))

    total = summed(2, my_xc, xc_peer)
    used = jnp.sum(counts_row[...].astype(F32))
    means = total / used
    loss[0] = means[0, 0]
    grad_bias[0] = means[0, 1]
    grad_log_temp[0] = means[0, 2]

    img_dir = img_dir + own_weight * txt_wide
    txt_dir = txt_dir + own_weight * img_wide
    for s in NEAR_FIRST:
        got_y[s].wait_recv()
        img_dir = img_dir + from_y[tile(s), :].astype(F32)
    img_dir = jnp.where(own_used > 0.0, img_dir, 0.0)
    grad_img[...] = projected(img_dir, img_unit, img_length)
    for s in NEAR_FIRST:
        got_z[s].wait_recv()
        txt_dir = txt_dir + from_z[tile(s), :].astype(F32)
    txt_dir = jnp.where(own_used > 0.0, txt_dir, 0.0)
    grad_txt[...] = projected(txt_dir, txt_unit, txt_length)

    for made in sent:
        made.wait_send()


def body(images, texts, row_counts, log_temp, bias):
    rows, width = images.shape
    scalar = jax.ShapeDtypeStruct((1,), F32)
    grad = jax.ShapeDtypeStruct((rows, width), F32)
    vmem = pl.BlockSpec(memory_space=pltpu.VMEM)
    smem = pl.BlockSpec(memory_space=pltpu.SMEM)
    return pl.pallas_call(
        kernel,
        out_shape=(scalar, scalar, scalar, grad, grad),
        in_specs=[vmem, vmem, smem, vmem, smem, smem],
        out_specs=(smem, smem, smem, vmem, vmem),
        scratch_shapes=[
            pltpu.VMEM((512, width), BF16),
            pltpu.VMEM((1024, width), BF16),
            pltpu.VMEM((1024, 512), BF16),
            pltpu.VMEM((256, 512), F32),
            pltpu.VMEM((1024, width), BF16),
            pltpu.VMEM((512, width), BF16),
            pltpu.VMEM((256, width), F32),
            pltpu.VMEM((256, width), F32),
            pltpu.VMEM((256, width), F32),
            pltpu.VMEM((512, width), BF16),
            pltpu.VMEM((256, width), BF16),
            pltpu.VMEM((256, width), BF16),
            pltpu.VMEM((256, width), BF16),
            pltpu.VMEM((256, width), BF16),
            pltpu.VMEM((3, 8, 8, 128), F32),
            pltpu.SemaphoreType.DMA((N_SEM,)),
            pltpu.SemaphoreType.DMA((N_SEM,)),
        ],
        compiler_params=pltpu.CompilerParams(
            collective_id=0, has_side_effects=True, vmem_limit_bytes=48 << 20
        ),
        cost_estimate=pl.CostEstimate(flops=6 * 512 * 1024 * width, bytes_accessed=4 << 20, transcendentals=1 << 20),
    )(images, texts, row_counts, row_counts.reshape(1, -1), log_temp, bias)


def solution(mesh):
    return jax.shard_map(
        body,
        mesh=mesh,
        in_specs=(P(("blk", "sub"), None), P(("blk", "sub"), None), P(), P(), P()),
        out_specs=(P(), P(), P(), P(("blk", "sub"), None), P(("blk", "sub"), None)),
        check_vma=False,
    )
```

```python
import functools

import jax
import jax.numpy as jnp
from jax import lax
from jax.experimental import pallas as pl
from jax.experimental.pallas import tpu as pltpu
from jax.sharding import PartitionSpec as P

MESH = pl.DeviceIdType.MESH
F32 = jnp.float32
BF16 = jnp.bfloat16
T = 32
RING = 8
N_SEM = 192
SCAL = 160
H0, H1 = (0, 16), (16, 16)
FULL = (0, T)


def place():
    blk, sub = lax.axis_index("blk"), lax.axis_index("sub")
    core = lax.rem(blk, 2)
    y = lax.rem(lax.div(blk, 2), RING)
    z = lax.rem(lax.div(blk, 16), 2) * 4 + sub
    x = lax.div(blk, 32)
    return x, y, z, core


def member(x, y, z, core):
    return ((x * 2 + lax.div(z, 4)) * RING + y) * 2 + core


def device(x, y, z, core):
    return (member(x, y, z, core), lax.rem(z, 4))


def ring(value):
    return lax.rem(value, RING)


def normalized(values):
    wide = values.astype(F32)
    length = jnp.sqrt(jnp.sum(wide * wide, axis=1, keepdims=True) + 1e-06)
    return wide / length, length


def projected(grad, unit, length):
    return (grad - unit * jnp.sum(unit * grad, axis=1, keepdims=True)) / length


def sigmoid_and_softplus(u):
    small = jnp.exp(-jnp.abs(u))
    ratio = 1.0 / (1.0 + small)
    sigmoid = jnp.where(u >= 0.0, ratio, small * ratio)
    softplus = jnp.maximum(u, 0.0) + jnp.log1p(small)
    return sigmoid, softplus


def at(slot, part=FULL):
    return pl.ds(slot * T + part[0], part[1])


def tile(slot):
    return pl.ds(slot * T, T)


def kernel(
    img_hbm, txt_hbm, counts_hbm, log_temp_hbm, bias_hbm,
    loss, grad_log_temp, grad_bias, grad_img, grad_txt,
    img_in, txt_in, counts, log_temp, bias, img, txt, weight, logits,
    out_c, from_c, img_sum, txt_sum, img_out, txt_out, img_back, txt_back, scal, local, ssem, rsem,
):
    x, y, z, core = place()
    pair_i = x + 1 - 2 * lax.rem(x, 2)
    pair_t = lax.rem(x + 3 + 2 * lax.rem(x, 2), 4)

    def y_peer(d):
        return device(x, ring(y + d), z, core)

    def z_peer(d):
        return device(x, y, ring(z + d), core)

    my_xc = x * 2 + core

    def xc_peer(d):
        other = ring(my_xc + d)
        return device(lax.div(other, 2), y, z, lax.rem(other, 2))

    img_mate = device(pair_i, y, z, core)
    txt_mate = device(pair_t, y, z, core)
    core_mate = device(x, y, z, 1 - core)

    barrier = pltpu.get_barrier_semaphore()
    for d in range(1, RING):
        for peer in (y_peer(d), z_peer(d), xc_peer(d)):
            pl.semaphore_signal(barrier, inc=1, device_id=peer, device_id_type=MESH)

    fetched = [
        pltpu.make_async_copy(source, target, local.at[k])
        for k, (source, target) in enumerate(
            ((counts_hbm, counts), (log_temp_hbm, log_temp), (bias_hbm, bias), (img_hbm, img_in), (txt_hbm, txt_in))
        )
    ]
    for made in fetched:
        made.start()
    for made in fetched:
        made.wait()

    temp = jnp.exp(jnp.full((1, 1), log_temp[0], F32))
    shift = bias[0]
    img_unit, img_length = normalized(img_in[...])
    txt_unit, txt_length = normalized(txt_in[...])

    def tile_used(x, y, z, core):
        return jnp.where(counts[member(x, y, z, core)] > T * lax.rem(z, 4), 1.0, 0.0)

    own_used = tile_used(x, y, z, core)
    img_half = jnp.where(own_used > 0.0, img_unit, 0.0).astype(BF16)
    txt_half = jnp.where(own_used > 0.0, txt_unit, 0.0).astype(BF16)
    img[tile(0), :] = img_half
    txt[tile(0), :] = txt_half

    sent = []

    def send(src, dst, peer):
        index = len(sent)
        made = pltpu.make_async_remote_copy(
            src_ref=src,
            dst_ref=dst,
            send_sem=ssem.at[index],
            recv_sem=rsem.at[index],
            device_id=peer,
            device_id_type=MESH,
        )
        made.start()
        sent.append(made)
        return made

    img_ring = (img, y_peer(1), y_peer(RING - 1), img_mate)
    txt_ring = (txt, z_peer(1), z_peer(RING - 1), txt_mate)
    rings = (txt_ring, img_ring)

    pl.semaphore_wait(barrier, 3 * (RING - 1))

    def across(which, slot, part):
        buf, _, _, mate = which
        return send(buf.at[at(slot, part)], buf.at[at(8 + slot, part)], mate)

    def forward(which, base, k, part):
        buf, plus, minus, _ = which
        return (
            send(buf.at[at(base + (RING - k + 1) % RING, part)], buf.at[at(base + RING - k, part)], plus),
            send(buf.at[at(base + k - 1, part)], buf.at[at(base + k, part)], minus),
        )

    def to_core(slot):
        return send(txt.at[at(slot)], txt.at[at(16 + slot)], core_mate)

    def last_whole(which):
        buf, plus, minus, _ = which
        return (
            send(buf.at[at(5, H0)], buf.at[at(4, H0)], plus),
            send(buf.at[at(3, H1)], buf.at[at(4, H1)], minus),
        )

    odd = lax.rem(core, 2)

    def toward(which):
        _, plus, minus, _ = which
        return (jnp.where(odd == 1, minus[0], plus[0]), jnp.where(odd == 1, minus[1], plus[1]))

    def last_half(which):
        buf = which[0]
        source = jnp.where(odd == 1, 8 + 3, 8 + 5)
        return (send(buf.at[pl.ds(pl.multiple_of(source * T, T), 16)], buf.at[at(12, H0)], toward(which)),)

    first = [across(r, 0, H0) for r in rings]
    whole = [forward(r, 0, 1, FULL) for r in rings]
    second = [{0: across(r, 0, H1)} for r in rings]
    core_got = [to_core(0)]

    img_wide, txt_wide = img_half.astype(F32), txt_half.astype(F32)
    own_u = temp * jnp.sum(img_wide * txt_wide, axis=1, keepdims=True) + shift
    own_sigmoid, own_softplus = sigmoid_and_softplus(-own_u)
    own_slope = -own_sigmoid * own_used
    own_pair = own_softplus * own_used
    own_weight = (own_slope * temp).astype(BF16).astype(F32)
    own_sums = (jnp.sum(own_pair), jnp.sum(own_slope), jnp.sum(own_slope * (own_u - shift)))

    halves = [(made,) for made in first]
    for k in range(1, 5):
        for n, r in enumerate(rings):
            for made in halves[n]:
                made.wait_recv()
            halves[n] = forward(r, 8, k, H0) if k < 4 else last_half(r)
        arrived = (RING - k, k) if k < 4 else (4,)
        for n, r in enumerate(rings):
            for made in whole[n]:
                made.wait_recv()
            if k < 3:
                whole[n] = forward(r, 0, k + 1, FULL)
            elif k == 3:
                whole[n] = last_whole(r)
            for s in arrived:
                second[n][s] = across(r, s, H1)
            if n == 0:
                core_got += [to_core(s) for s in arrived]
        for s in (RING - k + 1, k - 1) if k > 1 else (0,):
            second[0][s].wait_recv()
            core_got.append(to_core(8 + s))
    for n in range(2):
        for made in halves[n]:
            made.wait_recv()
    second[0][4].wait_recv()
    core_got.append(to_core(12))
    for made in second[1].values():
        made.wait_recv()
    for made in core_got:
        made.wait_recv()

    def block(c, sums):
        rows = pl.ds(pl.multiple_of(c * 256, 256), 256)
        logits[...] = lax.dot_general(
            txt[rows, :], img[...], (((1,), (1,)), ((), ())), preferred_element_type=F32
        )
        tx = jnp.where(lax.rem(c, 2) == 1, pair_t, x)
        tc = jnp.where(c >= 2, 1 - core, core)
        pair_sum, slope_sum, scaled_sum = sums
        for k in range(8):
            scaled = logits[tile(k), :] * temp
            u = scaled + shift
            slope, pair = sigmoid_and_softplus(u)
            if k == 0:
                row = lax.broadcasted_iota(jnp.int32, (T, 512), 0)
                column = lax.broadcasted_iota(jnp.int32, (T, 512), 1)
                own = (row == column) & (c == 0)
                slope = jnp.where(own, 0.0, slope)
                pair = jnp.where(own, 0.0, pair)
            weight[pl.ds(pl.multiple_of(c * 256 + k * T, T), T), :] = (slope * temp).astype(BF16)
            used = tile_used(tx, y, ring(z + k), tc)

            def folded(value):
                return jnp.sum(value.reshape(T // 8, 8, 512), axis=0)

            pair_sum = pair_sum + used * folded(pair)
            slope_sum = slope_sum + used * folded(slope)
            scaled_sum = scaled_sum + folded(slope * scaled)
        return pair_sum, slope_sum, scaled_sum

    zero = jnp.zeros((8, 512), F32)
    pair_sum, slope_sum, scaled_sum = lax.fori_loop(0, 4, block, (zero, zero, zero))

    column_tile = lax.broadcasted_iota(jnp.int32, (8, 512), 1) // T
    columns_used = zero
    for s in range(16):
        used = tile_used(x if s < 8 else pair_i, ring(y + s), z, core)
        columns_used = jnp.where(column_tile == s, used, columns_used)
    sums = (
        jnp.sum(pair_sum * columns_used) + own_sums[0],
        jnp.sum(slope_sum * columns_used) + own_sums[1],
        jnp.sum(scaled_sum) + own_sums[2],
    )
    lane = lax.broadcasted_iota(jnp.int32, (8, 128), 1)
    vector = jnp.where(lane == 0, sums[0], jnp.where(lane == 1, sums[1], jnp.where(lane == 2, sums[2], 0.0)))

    scal_sent = []

    def scalar_copy(stage, d, mine, slot, peer):
        return pltpu.make_async_remote_copy(
            src_ref=scal.at[stage, mine],
            dst_ref=scal.at[stage, slot],
            send_sem=ssem.at[SCAL + stage * 8 + d],
            recv_sem=rsem.at[SCAL + stage * 8 + slot],
            device_id=peer,
            device_id_type=MESH,
        )

    def spread(stage, mine, peer_of, value):
        scal[stage, mine] = value
        for d in range(1, RING):
            made = scalar_copy(stage, d, mine, mine, peer_of(d))
            made.start()
            scal_sent.append(made)

    def summed(stage, mine, peer_of):
        for d in range(1, RING):
            scalar_copy(stage, d, mine, ring(mine + d), peer_of(d)).wait_recv()
        total = scal[stage, 0]
        for k in range(1, RING):
            total = total + scal[stage, k]
        return total

    spread(0, y, y_peer, vector)

    def text_dir(first):
        return jnp.dot(weight[first : first + 256, :], img[...], preferred_element_type=F32)

    core_back = []
    for first in (256, 0):
        out_c[first : first + 256, :] = text_dir(512 + first).astype(BF16)
        part = pl.ds(first, 256)
        core_back.append(send(out_c.at[part], from_c.at[part], core_mate))
    for first in (256, 0):
        img_sum[first : first + 256, :] = lax.dot_general(
            weight[:, first : first + 256], txt[...], (((0,), (0,)), ((), ())), preferred_element_type=F32
        )
    for first in (256, 0):
        txt_sum[first : first + 256, :] = text_dir(first)

    total = summed(0, y, y_peer)
    spread(1, z, z_peer, total)

    for made in core_back:
        made.wait_recv()

    def img_own(slot, part):
        return img_sum[at(slot, part), :]

    def txt_own(slot, part):
        return txt_sum[at(slot, part), :] + from_c[at(slot, part), :].astype(F32)

    back = (
        (txt_own, txt_out, txt_back, z_peer(1), z_peer(RING - 1), txt_mate),
        (img_own, img_out, img_back, y_peer(1), y_peer(RING - 1), img_mate),
    )
    WHOLE, HALF, MATE, HOME = 0, 8 * T, 12 * T, 16 * T

    def landing(first, n):
        return pl.ds(first, n)

    def whole_place(way, k, part=FULL):
        return landing(WHOLE + (way * 4 + k - 1) * T + part[0], part[1])

    def half_place(way, k):
        return landing(HALF + (way * 4 + k - 1) * 16, 16)

    def mate_place(slot):
        return landing(MATE + slot * 16, 16)

    def emit(which, slot, part, value, place, peer):
        _, out, recv = which[:3]
        out[at(slot, part), :] = value.astype(BF16)
        return send(out.at[at(slot, part)], recv.at[place], peer)

    mate_got = [{}, {}]
    for s in (4, 3, 5, 2, 6, 1, 7, 0):
        for n, r in enumerate(back):
            mate_got[n][s] = emit(r, 8 + s, H1, r[0](8 + s, H1), mate_place(s), r[5])

    half_got, whole_got = [None, None], [None, None]
    for n, r in enumerate(back):
        way = toward((None, r[3], r[4], None))
        made = emit(r, 12, H0, r[0](12, H0), half_place(0, 1), way)
        half_got[n] = (made,)
    up = [emit(r, 4, H0, r[0](4, H0), whole_place(0, 1, H0), r[3]) for r in back]

    def from_mate(n, s):
        mate_got[n][s].wait_recv()
        return back[n][0](s, H1) + back[n][2][mate_place(s), :].astype(F32)

    for n, r in enumerate(back):
        down = emit(r, 4, H1, from_mate(n, 4), whole_place(1, 1, H1), r[4])
        whole_got[n] = (up[n], down)

    for k in range(2, 5):
        for n, r in enumerate(back):
            for made in half_got[n]:
                made.wait_recv()
            made = []
            for way, s in enumerate((5 - k, 3 + k)):
                value = r[0](8 + s, H0)
                if k == 2:
                    value = value + jnp.where(odd == way, r[2][half_place(0, 1), :].astype(F32), 0.0)
                else:
                    value = value + r[2][half_place(way, k - 1), :].astype(F32)
                made.append(emit(r, 8 + s, H0, value, half_place(way, k), r[3 + way]))
            half_got[n] = made
        for n, r in enumerate(back):
            made = []
            for way, s in enumerate((5 - k, 3 + k)):
                top, low = r[0](s, H0), from_mate(n, s)
                whole_got[n][way].wait_recv()
                if k > 2 or way == 0:
                    top = top + r[2][whole_place(way, k - 1, H0), :].astype(F32)
                if k > 2 or way == 1:
                    low = low + r[2][whole_place(way, k - 1, H1), :].astype(F32)
                r[1][at(s, H0), :] = top.astype(BF16)
                r[1][at(s, H1), :] = low.astype(BF16)
                made.append(send(r[1].at[at(s)], r[2].at[whole_place(way, k)], r[3 + way]))
            whole_got[n] = made
        if k == 2:
            total = summed(1, z, z_peer)
            spread(2, my_xc, xc_peer, total)

    home = []
    for n, r in enumerate(back):
        value = r[0](8, H0)
        for way in range(2):
            half_got[n][way].wait_recv()
            value = value + r[2][half_place(way, 4), :].astype(F32)
        home.append(emit(r, 8, H0, value, landing(HOME, 16), r[5]))

    total = summed(2, my_xc, xc_peer)
    used = lax.fori_loop(0, counts.shape[0], lambda i, sum: sum + counts[i], 0).astype(F32)
    means = total / used
    loss[0] = means[0, 0]
    grad_bias[0] = means[0, 1]
    grad_log_temp[0] = means[0, 2]

    ends = ((txt_unit, txt_length, img_wide, grad_txt), (img_unit, img_length, txt_wide, grad_img))
    for n, r in enumerate(back):
        unit, length, other, grad = ends[n]
        top, low = r[0](0, H0), from_mate(n, 0)
        for way in range(2):
            whole_got[n][way].wait_recv()
            top = top + r[2][whole_place(way, 4, H0), :].astype(F32)
            low = low + r[2][whole_place(way, 4, H1), :].astype(F32)
        home[n].wait_recv()
        top = top + r[2][landing(HOME, 16), :].astype(F32)
        total_dir = jnp.concatenate([top, low], axis=0) + own_weight * other
        total_dir = jnp.where(own_used > 0.0, total_dir, 0.0)
        grad[...] = projected(total_dir, unit, length)

    assert len(sent) <= SCAL
    for made in sent + scal_sent:
        made.wait_send()


def place_results(*refs):
    sources, targets, arrived = refs[:5], refs[5:10], refs[10]
    moved = [pltpu.make_async_copy(sources[k], targets[k], arrived.at[k]) for k in range(5)]
    for made in moved:
        made.start()
    for made in moved:
        made.wait()


def body(images, texts, row_counts, log_temp, bias):
    rows, width = images.shape
    scalar = jax.ShapeDtypeStruct((1,), F32)
    grad = jax.ShapeDtypeStruct((rows, width), F32)
    vmem = pl.BlockSpec(memory_space=pltpu.VMEM)
    smem = pl.BlockSpec(memory_space=pltpu.SMEM)
    found = pl.pallas_call(
        kernel,
        out_shape=(scalar, scalar, scalar, grad, grad),
        in_specs=[pl.BlockSpec(memory_space=pltpu.HBM)] * 5,
        out_specs=(smem, smem, smem, vmem, vmem),
        scratch_shapes=[
            pltpu.VMEM((T, width), BF16),
            pltpu.VMEM((T, width), BF16),
            pltpu.SMEM(row_counts.shape, jnp.int32),
            pltpu.SMEM((1,), F32),
            pltpu.SMEM((1,), F32),
            pltpu.VMEM((512, width), BF16),
            pltpu.VMEM((1024, width), BF16),
            pltpu.VMEM((1024, 512), BF16),
            pltpu.VMEM((256, 512), F32),
            pltpu.VMEM((512, width), BF16),
            pltpu.VMEM((512, width), BF16),
            pltpu.VMEM((512, width), F32),
            pltpu.VMEM((512, width), F32),
            pltpu.VMEM((512, width), BF16),
            pltpu.VMEM((512, width), BF16),
            pltpu.VMEM((17 * T, width), BF16),
            pltpu.VMEM((17 * T, width), BF16),
            pltpu.VMEM((3, 8, 8, 128), F32),
            pltpu.SemaphoreType.DMA((5,)),
            pltpu.SemaphoreType.DMA((N_SEM,)),
            pltpu.SemaphoreType.DMA((N_SEM,)),
        ],
        compiler_params=pltpu.CompilerParams(
            collective_id=0, has_side_effects=True, vmem_limit_bytes=60 << 20
        ),
        cost_estimate=pl.CostEstimate(flops=6 * 512 * 1024 * width, bytes_accessed=4 << 20, transcendentals=1 << 20),
    )(images, texts, row_counts, log_temp, bias)
    return pl.pallas_call(
        place_results,
        out_shape=(scalar, scalar, scalar, grad, grad),
        in_specs=[smem] * 3 + [vmem] * 2,
        out_specs=[pl.BlockSpec(memory_space=pltpu.HBM)] * 5,
        scratch_shapes=[pltpu.SemaphoreType.DMA((5,))],
    )(*found)


def solution(mesh):
    return jax.shard_map(
        body,
        mesh=mesh,
        in_specs=(P(("blk", "sub"), None), P(("blk", "sub"), None), P(), P(), P()),
        out_specs=(P(), P(), P(), P(("blk", "sub"), None), P(("blk", "sub"), None)),
        check_vma=False,
    )
```

```python
import functools

import jax
import jax.numpy as jnp
from jax import lax
from jax.experimental import pallas as pl
from jax.experimental.pallas import tpu as pltpu
from jax.sharding import PartitionSpec as P

MESH = pl.DeviceIdType.MESH
F32 = jnp.float32
BF16 = jnp.bfloat16
T = 32
RING = 8
N_SEM = 192
SCAL = 160
FULL = (0, T)
PIECES = ((0, 16), (16, 16))
OWN, MATE = 0, 1
ROUTES = (
    ({1: 0, 2: 0, 3: 2, 4: 3}, {0: None, 1: None, 2: None, 3: None, 4: 2}),
    ({1: 0, 2: 1, 3: 2, 4: 2}, {0: None, 1: 0, 2: None, 3: 1, 4: 3}),
)
CORE = 2
GATHER = (
    (MATE, 1, 0), (OWN, 1, 1), (OWN, 0, 2), (OWN, 0, 1), (MATE, 0, 0), (CORE, OWN, 0), (MATE, 1, 1), (CORE, MATE, 0),
    (OWN, 1, 2), (MATE, 0, 1), (OWN, 0, 3), (MATE, 0, 2), (CORE, OWN, 1), (MATE, 1, 3), (OWN, 1, 3), (OWN, 1, 4),
    (MATE, 1, 2), (CORE, OWN, 2), (MATE, 0, 3), (OWN, 0, 4), (CORE, MATE, 1), (MATE, 0, 4), (MATE, 1, 4),
    (CORE, OWN, 3), (CORE, MATE, 2), (CORE, OWN, 4), (CORE, MATE, 3), (CORE, MATE, 4),
)
REDUCE = (
    (MATE, 0, 4), (MATE, 1, 4), (MATE, 0, 3), (OWN, 0, 4), (MATE, 1, 2), (OWN, 1, 3), (OWN, 1, 4), (MATE, 1, 3),
    (MATE, 0, 2), (MATE, 0, 1), (OWN, 0, 3), (OWN, 1, 2), (MATE, 1, 1), (OWN, 0, 2), (OWN, 0, 1), (OWN, 1, 1),
    (MATE, 1, 0), (MATE, 0, 0),
)
ORDER = (12, 11, 13, 4, 10, 14, 5, 3, 9, 15, 6, 2, 7, 1, 8, 0)


def ways(k):
    return (0, 1) if 0 < k < 4 else (0,)


def ring_slot(k, way):
    return (RING - k) % RING if way == 0 else k


def place():
    blk, sub = lax.axis_index("blk"), lax.axis_index("sub")
    core = lax.rem(blk, 2)
    y = lax.rem(lax.div(blk, 2), RING)
    z = lax.rem(lax.div(blk, 16), 2) * 4 + sub
    x = lax.div(blk, 32)
    return x, y, z, core


def member(x, y, z, core):
    return ((x * 2 + lax.div(z, 4)) * RING + y) * 2 + core


def device(x, y, z, core):
    return (member(x, y, z, core), lax.rem(z, 4))


def ring(value):
    return lax.rem(value, RING)


def normalized(values):
    wide = values.astype(F32)
    length = jnp.sqrt(jnp.sum(wide * wide, axis=1, keepdims=True) + 1e-06)
    return wide / length, length


def projected(grad, unit, length):
    return (grad - unit * jnp.sum(unit * grad, axis=1, keepdims=True)) / length


def sigmoid_and_softplus(u):
    small = jnp.exp(-jnp.abs(u))
    ratio = 1.0 / (1.0 + small)
    sigmoid = jnp.where(u >= 0.0, ratio, small * ratio)
    softplus = jnp.maximum(u, 0.0) + jnp.log1p(small)
    return sigmoid, softplus


def at(slot, part=FULL):
    return pl.ds((slot // 16 * 16 + ORDER.index(slot % 16)) * T + part[0], part[1])


def tile(slot):
    return pl.ds(slot * T, T)


def kernel(
    img_hbm, txt_hbm, counts_hbm, log_temp_hbm, bias_hbm,
    loss, grad_log_temp, grad_bias, grad_img, grad_txt,
    img_in, txt_in, counts, log_temp, bias, img, txt, weight, logits,
    out_c, from_c, img_sum, txt_sum, img_out, txt_out, img_back, txt_back, scal, local, ssem, rsem,
):
    x, y, z, core = place()
    pair_i = x + 1 - 2 * lax.rem(x, 2)
    pair_t = lax.rem(x + 3 + 2 * lax.rem(x, 2), 4)

    def y_peer(d):
        return device(x, ring(y + RING + d), z, core)

    def z_peer(d):
        return device(x, y, ring(z + RING + d), core)

    my_xc = x * 2 + core

    def xc_peer(d):
        other = ring(my_xc + d)
        return device(lax.div(other, 2), y, z, lax.rem(other, 2))

    img_mate = device(pair_i, y, z, core)
    txt_mate = device(pair_t, y, z, core)
    core_mate = device(x, y, z, 1 - core)

    fetched = [
        pltpu.make_async_copy(source, target, local.at[k])
        for k, (source, target) in enumerate(
            ((counts_hbm, counts), (log_temp_hbm, log_temp), (bias_hbm, bias), (img_hbm, img_in), (txt_hbm, txt_in))
        )
    ]
    for made in fetched:
        made.start()

    barrier = pltpu.get_barrier_semaphore()
    for d in range(1, RING):
        for peer in (y_peer(d), z_peer(d), xc_peer(d)):
            pl.semaphore_signal(barrier, inc=1, device_id=peer, device_id_type=MESH)

    for made in fetched:
        made.wait()

    temp = jnp.exp(jnp.full((1, 1), log_temp[0], F32))
    shift = bias[0]
    img_unit, img_length = normalized(img_in[...])
    txt_unit, txt_length = normalized(txt_in[...])

    def tile_used(x, y, z, core):
        return jnp.where(counts[member(x, y, z, core)] > T * lax.rem(z, 4), 1.0, 0.0)

    own_used = tile_used(x, y, z, core)
    img_half = jnp.where(own_used > 0.0, img_unit, 0.0).astype(BF16)
    txt_half = jnp.where(own_used > 0.0, txt_unit, 0.0).astype(BF16)
    img[at(0), :] = img_half
    txt[at(0), :] = txt_half

    sent = []

    def send(src, dst, peer):
        index = len(sent)
        made = pltpu.make_async_remote_copy(
            src_ref=src,
            dst_ref=dst,
            send_sem=ssem.at[index],
            recv_sem=rsem.at[index],
            device_id=peer,
            device_id_type=MESH,
        )
        made.start()
        sent.append(made)
        return made

    odd = lax.rem(core, 2)
    TXT, IMG = 0, 1
    ring_buf, ring_peer, ring_mate = (txt, img), (z_peer, y_peer), (txt_mate, img_mate)

    pl.semaphore_wait(barrier, 3 * (RING - 1))

    gathered = {}

    def way_on(ring, k, parent):
        return ring_peer[ring](jnp.where(odd == 1, parent - k, k - parent))

    def move(ring, column, piece, k):
        buf, part = ring_buf[ring], PIECES[piece]
        parent, made = ROUTES[piece][column][k], []
        for way in ways(k):
            slot = ring_slot(k, way)
            if parent is None:
                source, target, peer = at(slot, part), at(8 + slot, part), ring_mate[ring]
            elif k < 4:
                source, target = at(column * 8 + ring_slot(parent, way), part), at(column * 8 + slot, part)
                peer = ring_peer[ring]((k - parent) * (1 - 2 * way))
            else:
                up, down = (ORDER.index(column * 8 + ring_slot(parent, w)) for w in (0, 1))
                first = jnp.where(odd == 1, down, up) * T + part[0]
                source, target = pl.ds(pl.multiple_of(first, 16), 16), at(column * 8 + slot, part)
                peer = way_on(ring, k, parent)
            made.append(send(buf.at[source], buf.at[target], peer))
        gathered[ring, column, piece, k] = made

    def arrive(*key):
        for made in gathered.get(key, ()):
            made.wait_recv()
        gathered[key] = ()

    def run(column, piece, k):
        if column == CORE:
            base = piece * 8
            if k or base:
                for n in range(2):
                    arrive(TXT, piece, n, k)
            gathered[TXT, CORE, piece, k] = [
                send(txt.at[at(base + ring_slot(k, way))], txt.at[at(16 + base + ring_slot(k, way))], core_mate)
                for way in ways(k)
            ]
            return
        parent = ROUTES[piece][column][k]
        for n in (TXT, IMG):
            if parent is None and k:
                arrive(n, OWN, piece, k)
            elif parent is not None and (parent or column == MATE):
                arrive(n, column, piece, parent)
            move(n, column, piece, k)

    at_once = 6
    for entry in GATHER[:at_once]:
        run(*entry)

    img_wide, txt_wide = img_half.astype(F32), txt_half.astype(F32)
    own_u = temp * jnp.sum(img_wide * txt_wide, axis=1, keepdims=True) + shift
    own_sigmoid, own_softplus = sigmoid_and_softplus(-own_u)
    own_slope = -own_sigmoid * own_used
    own_pair = own_softplus * own_used
    own_weight = (own_slope * temp).astype(BF16).astype(F32)
    own_sums = [jnp.sum(value, axis=0, keepdims=True) for value in (own_pair, own_slope, own_slope * (own_u - shift))]
    used = lax.fori_loop(0, counts.shape[0], lambda i, sum: sum + counts[i], 0).astype(F32)

    column_tile = lax.broadcasted_iota(jnp.int32, (8, 512), 1) // T
    columns_used = jnp.zeros((8, 512), F32)
    for k, s in enumerate(ORDER):
        columns_used = jnp.where(
            column_tile == k, tile_used(x if s < 8 else pair_i, ring(y + s), z, core), columns_used
        )

    for entry in GATHER[at_once:]:
        run(*entry)
    for key in tuple(gathered):
        arrive(*key)

    def block(c, sums):
        rows = pl.ds(pl.multiple_of(c * 256, 256), 256)
        logits[...] = lax.dot_general(
            txt[rows, :], img[...], (((1,), (1,)), ((), ())), preferred_element_type=F32
        )
        late = lax.rem(c, 2) == 1
        tc = jnp.where(c >= 2, 1 - core, core)
        pair_sum, slope_sum, scaled_sum = sums
        for k in range(8):
            scaled = logits[tile(k), :] * temp
            u = scaled + shift
            slope, pair = sigmoid_and_softplus(u)
            if k == 7:
                row = lax.broadcasted_iota(jnp.int32, (T, 512), 0)
                column = lax.broadcasted_iota(jnp.int32, (T, 512), 1)
                own = (row + 15 * T == column) & (c == 1)
                slope = jnp.where(own, 0.0, slope)
                pair = jnp.where(own, 0.0, pair)
            weight[pl.ds(pl.multiple_of(c * 256 + k * T, T), T), :] = (slope * temp).astype(BF16)
            slot = jnp.where(late, ORDER[8 + k], ORDER[k])
            used = tile_used(jnp.where(slot >= 8, pair_t, x), y, ring(z + slot), tc)

            def folded(value):
                return jnp.sum(value.reshape(T // 8, 8, 512), axis=0)

            pair_sum = pair_sum + used * folded(pair)
            slope_sum = slope_sum + used * folded(slope)
            scaled_sum = scaled_sum + folded(slope * scaled)
        return pair_sum, slope_sum, scaled_sum

    zero = jnp.zeros((8, 512), F32)
    pair_sum, slope_sum, scaled_sum = lax.fori_loop(0, 4, block, (zero, zero, zero))

    lane = lax.broadcasted_iota(jnp.int32, (8, 128), 1)

    def own_total():
        whole = [
            jnp.sum(value, axis=(0, 1), keepdims=True)
            for value in (pair_sum * columns_used, slope_sum * columns_used, scaled_sum)
        ]
        vector = jnp.zeros((8, 128), F32)
        for k in range(3):
            vector = jnp.where(lane == k, whole[k] + own_sums[k], vector)
        return vector

    scal_sent = []

    def scalar_copy(stage, d, mine, slot, peer):
        return pltpu.make_async_remote_copy(
            src_ref=scal.at[stage, mine],
            dst_ref=scal.at[stage, slot],
            send_sem=ssem.at[SCAL + stage * 8 + d],
            recv_sem=rsem.at[SCAL + stage * 8 + slot],
            device_id=peer,
            device_id_type=MESH,
        )

    def spread(stage, mine, peer_of, value):
        scal[stage, mine] = value
        for d in range(1, RING):
            made = scalar_copy(stage, d, mine, mine, peer_of(d))
            made.start()
            scal_sent.append(made)

    def summed(stage, mine, peer_of):
        for d in range(1, RING):
            scalar_copy(stage, d, mine, ring(mine + d), peer_of(d)).wait_recv()
        total = scal[stage, 0]
        for k in range(1, RING):
            total = total + scal[stage, k]
        return total

    def rows_of(group):
        return pl.ds(group * 128, 128)

    def text_dir(first):
        return jnp.dot(weight[first : first + 128, :], img[...], preferred_element_type=F32)

    core_back = {}

    def other_texts(group):
        out_c[rows_of(group), :] = text_dir(512 + group * 128).astype(BF16)
        core_back[group] = send(out_c.at[rows_of(group)], from_c.at[rows_of(group)], core_mate)

    def own_images(group):
        img_sum[rows_of(group), :] = lax.dot_general(
            weight[:, group * 128 : group * 128 + 128], txt[...], (((0,), (0,)), ((), ())), preferred_element_type=F32
        )

    def own_texts(group):
        txt_sum[rows_of(group), :] = text_dir(group * 128)

    computed = set()

    def compute(group):
        if group not in computed:
            computed.add(group)
            if group == 0:
                other_texts(0)
            own_images(group)
            if group < 3:
                other_texts(group + 1)
            own_texts(group)

    core_seen = set()

    def own_part(ring, slot, part):
        group = ORDER.index(slot) // 4
        compute(group)
        if ring == IMG:
            return img_sum[at(slot, part), :]
        if group not in core_seen:
            core_seen.add(group)
            core_back[group].wait_recv()
        return txt_sum[at(slot, part), :] + from_c[at(slot, part), :].astype(F32)

    out, back = (txt_out, img_out), (txt_back, img_back)
    coming, places = {}, {}

    def landing(column, piece, k, way):
        row = places.setdefault((column, piece, k, way), len(places) * 16)
        return pl.ds(row, 16)

    def received(ring, column, piece, k, way):
        key = (ring, column, piece, k, way)
        if coming[key] is not None:
            coming[key].wait_recv()
            coming[key] = None
        return back[ring][landing(column, piece, k, way), :].astype(F32)

    def partial(ring, column, piece, k, way):
        value = own_part(ring, column * 8 + ring_slot(k, way), PIECES[piece])
        if column == OWN and ROUTES[piece][MATE][k] is None:
            value = value + received(ring, MATE, piece, k, way)
        for further, parent in ROUTES[piece][column].items():
            if parent != k:
                continue
            if further < 4:
                for w in (0, 1) if k == 0 else (way,):
                    value = value + received(ring, column, piece, further, w)
            else:
                extra = received(ring, column, piece, 4, 0)
                value = value + (extra if k == 0 else jnp.where(odd == way, extra, 0.0))
        return value

    def pass_back(ring, column, piece, k):
        parent, part = ROUTES[piece][column][k], PIECES[piece]
        for way in ways(k):
            slot = column * 8 + ring_slot(k, way)
            out[ring][at(slot, part), :] = partial(ring, column, piece, k, way).astype(BF16)
            if parent is None:
                peer = ring_mate[ring]
            elif k < 4:
                peer = ring_peer[ring]((parent - k) * (1 - 2 * way))
            else:
                peer = ring_peer[ring](jnp.where(odd == 1, k - parent, parent - k))
            target = back[ring].at[landing(column, piece, k, way)]
            coming[ring, column, piece, k, way] = send(out[ring].at[at(slot, part)], target, peer)

    for n, entry in enumerate(REDUCE):
        for which in (IMG, TXT):
            pass_back(which, *entry)
        if n == 1:
            spread(0, y, y_peer, own_total())
        elif n == 8:
            spread(1, z, z_peer, summed(0, y, y_peer))
        elif n == 13:
            spread(2, my_xc, xc_peer, summed(1, z, z_peer))

    total = summed(2, my_xc, xc_peer)
    means = total / used
    loss[0] = means[0, 0]
    grad_bias[0] = means[0, 1]
    grad_log_temp[0] = means[0, 2]

    ends = ((txt_unit, txt_length, img_wide, grad_txt), (img_unit, img_length, txt_wide, grad_img))
    for n in (TXT, IMG):
        unit, length, other, grad = ends[n]
        top, low = (partial(n, OWN, piece, 0, 0) for piece in (0, 1))
        total_dir = jnp.concatenate([top, low], axis=0) + own_weight * other
        total_dir = jnp.where(own_used > 0.0, total_dir, 0.0)
        grad[...] = projected(total_dir, unit, length)

    assert len(sent) <= SCAL and len(places) * 16 <= back[0].shape[0]
    for made in sent + scal_sent:
        made.wait_send()


def place_results(*refs):
    sources, targets, arrived = refs[:5], refs[5:10], refs[10]
    moved = [pltpu.make_async_copy(sources[k], targets[k], arrived.at[k]) for k in range(5)]
    for made in moved:
        made.start()
    for made in moved:
        made.wait()


def body(images, texts, row_counts, log_temp, bias):
    rows, width = images.shape
    scalar = jax.ShapeDtypeStruct((1,), F32)
    grad = jax.ShapeDtypeStruct((rows, width), F32)
    vmem = pl.BlockSpec(memory_space=pltpu.VMEM)
    smem = pl.BlockSpec(memory_space=pltpu.SMEM)
    found = pl.pallas_call(
        kernel,
        out_shape=(scalar, scalar, scalar, grad, grad),
        in_specs=[pl.BlockSpec(memory_space=pltpu.HBM)] * 5,
        out_specs=(smem, smem, smem, vmem, vmem),
        scratch_shapes=[
            pltpu.VMEM((T, width), BF16),
            pltpu.VMEM((T, width), BF16),
            pltpu.SMEM(row_counts.shape, jnp.int32),
            pltpu.SMEM((1,), F32),
            pltpu.SMEM((1,), F32),
            pltpu.VMEM((512, width), BF16),
            pltpu.VMEM((1024, width), BF16),
            pltpu.VMEM((1024, 512), BF16),
            pltpu.VMEM((256, 512), F32),
            pltpu.VMEM((512, width), BF16),
            pltpu.VMEM((512, width), BF16),
            pltpu.VMEM((512, width), F32),
            pltpu.VMEM((512, width), F32),
            pltpu.VMEM((512, width), BF16),
            pltpu.VMEM((512, width), BF16),
            pltpu.VMEM((480, width), BF16),
            pltpu.VMEM((480, width), BF16),
            pltpu.VMEM((3, 8, 8, 128), F32),
            pltpu.SemaphoreType.DMA((5,)),
            pltpu.SemaphoreType.DMA((N_SEM,)),
            pltpu.SemaphoreType.DMA((N_SEM,)),
        ],
        compiler_params=pltpu.CompilerParams(
            collective_id=0, has_side_effects=True, vmem_limit_bytes=60 << 20
        ),
        cost_estimate=pl.CostEstimate(flops=6 * 512 * 1024 * width, bytes_accessed=4 << 20, transcendentals=1 << 20),
    )(images, texts, row_counts, log_temp, bias)
    return pl.pallas_call(
        place_results,
        out_shape=(scalar, scalar, scalar, grad, grad),
        in_specs=[smem] * 3 + [vmem] * 2,
        out_specs=[pl.BlockSpec(memory_space=pltpu.HBM)] * 5,
        scratch_shapes=[pltpu.SemaphoreType.DMA((5,))],
    )(*found)


def solution(mesh):
    return jax.shard_map(
        body,
        mesh=mesh,
        in_specs=(P(("blk", "sub"), None), P(("blk", "sub"), None), P(), P(), P()),
        out_specs=(P(), P(), P(), P(("blk", "sub"), None), P(("blk", "sub"), None)),
        check_vma=False,
    )
```

```python
import functools

import jax
import jax.numpy as jnp
from jax import lax
from jax.experimental import pallas as pl
from jax.experimental.pallas import tpu as pltpu
from jax.sharding import PartitionSpec as P

MESH = pl.DeviceIdType.MESH
F32 = jnp.float32
BF16 = jnp.bfloat16
T = 32
RING = 8
N_SEM = 192
SCAL = 160
FULL = (0, T)
PIECES = ((0, 16), (16, 16))
OWN, MATE = 0, 1
ROUTES = (
    ({1: 0, 2: 0, 3: 2, 4: 3}, {0: None, 1: None, 2: None, 3: None, 4: 2}),
    ({1: 0, 2: 1, 3: 2, 4: 2}, {0: None, 1: 0, 2: None, 3: 1, 4: 3}),
)
CORE = 2
GATHER = (
    (MATE, 1, 0), (OWN, 1, 1), (OWN, 0, 2), (OWN, 0, 1), (MATE, 0, 0), (CORE, OWN, 0), (MATE, 1, 1), (CORE, MATE, 0),
    (OWN, 1, 2), (MATE, 0, 1), (OWN, 0, 3), (MATE, 0, 2), (CORE, OWN, 1), (MATE, 1, 3), (OWN, 1, 3), (OWN, 1, 4),
    (MATE, 1, 2), (CORE, OWN, 2), (MATE, 0, 3), (OWN, 0, 4), (CORE, MATE, 1), (MATE, 0, 4), (MATE, 1, 4),
    (CORE, OWN, 3), (CORE, MATE, 2), (CORE, OWN, 4), (CORE, MATE, 3), (CORE, MATE, 4),
)
REDUCE = (
    (MATE, 0, 4), (MATE, 1, 4), (MATE, 0, 3), (OWN, 0, 4), (MATE, 1, 2), (OWN, 1, 3), (OWN, 1, 4), (MATE, 1, 3),
    (MATE, 0, 2), (MATE, 0, 1), (OWN, 0, 3), (OWN, 1, 2), (MATE, 1, 1), (OWN, 0, 2), (OWN, 0, 1), (OWN, 1, 1),
    (MATE, 1, 0), (MATE, 0, 0),
)
ORDER = (12, 11, 13, 4, 10, 14, 5, 3, 9, 15, 6, 2, 7, 1, 8, 0)


def ways(k):
    return (0, 1) if 0 < k < 4 else (0,)


def ring_slot(k, way):
    return (RING - k) % RING if way == 0 else k


def place():
    blk, sub = lax.axis_index("blk"), lax.axis_index("sub")
    core = lax.rem(blk, 2)
    y = lax.rem(lax.div(blk, 2), RING)
    z = lax.rem(lax.div(blk, 16), 2) * 4 + sub
    x = lax.div(blk, 32)
    return x, y, z, core


def member(x, y, z, core):
    return ((x * 2 + lax.div(z, 4)) * RING + y) * 2 + core


def device(x, y, z, core):
    return (member(x, y, z, core), lax.rem(z, 4))


def ring(value):
    return lax.rem(value, RING)


def normalized(values):
    wide = values.astype(F32)
    length = jnp.sqrt(jnp.sum(wide * wide, axis=1, keepdims=True) + 1e-06)
    return wide / length, length


def projected(grad, unit, length):
    return (grad - unit * jnp.sum(unit * grad, axis=1, keepdims=True)) / length


def sigmoid_and_softplus(u):
    small = jnp.exp(-jnp.abs(u))
    ratio = 1.0 / (1.0 + small)
    sigmoid = jnp.where(u >= 0.0, ratio, small * ratio)
    softplus = jnp.maximum(u, 0.0) + jnp.log1p(small)
    return sigmoid, softplus


def at(slot, part=FULL):
    return pl.ds((slot // 16 * 16 + ORDER.index(slot % 16)) * T + part[0], part[1])


def tile(slot):
    return pl.ds(slot * T, T)


def kernel(
    img_hbm, txt_hbm, counts_hbm, log_temp_hbm, bias_hbm,
    scalars, grad_img, grad_txt,
    img_in, txt_in, counts, log_temp, bias, img, txt, weight, logits,
    out_c, from_c, img_sum, txt_sum, img_out, txt_out, img_back, txt_back, scal, local, ssem, rsem,
):
    x, y, z, core = place()
    pair_i = x + 1 - 2 * lax.rem(x, 2)
    pair_t = lax.rem(x + 3 + 2 * lax.rem(x, 2), 4)

    def y_peer(d):
        return device(x, ring(y + RING + d), z, core)

    def z_peer(d):
        return device(x, y, ring(z + RING + d), core)

    my_xc = x * 2 + core

    def xc_peer(d):
        other = ring(my_xc + d)
        return device(lax.div(other, 2), y, z, lax.rem(other, 2))

    img_mate = device(pair_i, y, z, core)
    txt_mate = device(pair_t, y, z, core)
    core_mate = device(x, y, z, 1 - core)

    fetched = [
        pltpu.make_async_copy(source, target, local.at[k])
        for k, (source, target) in enumerate(
            ((txt_hbm, txt_in), (img_hbm, img_in), (counts_hbm, counts), (log_temp_hbm, log_temp), (bias_hbm, bias))
        )
    ]
    for made in fetched:
        made.start()

    barrier = pltpu.get_barrier_semaphore()
    for d in range(1, RING):
        for peer in (y_peer(d), z_peer(d), xc_peer(d)):
            pl.semaphore_signal(barrier, inc=1, device_id=peer, device_id_type=MESH)

    def tile_used(x, y, z, core):
        return jnp.where(counts[member(x, y, z, core)] > T * lax.rem(z, 4), 1.0, 0.0)

    fetched[0].wait()
    txt_unit, txt_length = normalized(txt_in[...])
    txt_half = txt_unit.astype(BF16)
    txt[at(0), :] = txt_half

    sent = []

    def send(src, dst, peer):
        index = len(sent)
        made = pltpu.make_async_remote_copy(
            src_ref=src,
            dst_ref=dst,
            send_sem=ssem.at[index],
            recv_sem=rsem.at[index],
            device_id=peer,
            device_id_type=MESH,
        )
        made.start()
        sent.append(made)
        return made

    odd = lax.rem(core, 2)
    TXT, IMG = 0, 1
    ring_buf, ring_peer, ring_mate = (txt, img), (z_peer, y_peer), (txt_mate, img_mate)

    pl.semaphore_wait(barrier, 3 * (RING - 1))

    gathered = {}

    def way_on(ring, k, parent):
        return ring_peer[ring](jnp.where(odd == 1, parent - k, k - parent))

    def move(ring, column, piece, k):
        buf, part = ring_buf[ring], PIECES[piece]
        parent, made = ROUTES[piece][column][k], []
        for way in ways(k):
            slot = ring_slot(k, way)
            if parent is None:
                source, target, peer = at(slot, part), at(8 + slot, part), ring_mate[ring]
            elif k < 4:
                source, target = at(column * 8 + ring_slot(parent, way), part), at(column * 8 + slot, part)
                peer = ring_peer[ring]((k - parent) * (1 - 2 * way))
            else:
                up, down = (ORDER.index(column * 8 + ring_slot(parent, w)) for w in (0, 1))
                first = jnp.where(odd == 1, down, up) * T + part[0]
                source, target = pl.ds(pl.multiple_of(first, 16), 16), at(column * 8 + slot, part)
                peer = way_on(ring, k, parent)
            made.append(send(buf.at[source], buf.at[target], peer))
        gathered[ring, column, piece, k] = made

    def arrive(*key):
        for made in gathered.get(key, ()):
            made.wait_recv()
        gathered[key] = ()

    def run(column, piece, k, rings=(0, 1)):
        if column == CORE:
            if TXT not in rings:
                return
            base = piece * 8
            if k or base:
                for n in range(2):
                    arrive(TXT, piece, n, k)
            gathered[TXT, CORE, piece, k] = [
                send(txt.at[at(base + ring_slot(k, way))], txt.at[at(16 + base + ring_slot(k, way))], core_mate)
                for way in ways(k)
            ]
            return
        parent = ROUTES[piece][column][k]
        for n in rings:
            if parent is None and k:
                arrive(n, OWN, piece, k)
            elif parent is not None and (parent or column == MATE):
                arrive(n, column, piece, parent)
            move(n, column, piece, k)

    at_once = 6
    for entry in GATHER[:at_once]:
        run(*entry, rings=(TXT,))
    fetched[1].wait()
    img_unit, img_length = normalized(img_in[...])
    img_half = img_unit.astype(BF16)
    img[at(0), :] = img_half
    for entry in GATHER[:at_once]:
        run(*entry, rings=(IMG,))
    for made in fetched[2:]:
        made.wait()
    own_used = tile_used(x, y, z, core)
    temp = jnp.exp(jnp.full((1, 1), log_temp[0], F32))
    shift = bias[0]

    img_wide, txt_wide = img_half.astype(F32), txt_half.astype(F32)
    own_u = temp * jnp.sum(img_wide * txt_wide, axis=1, keepdims=True) + shift
    own_sigmoid, own_softplus = sigmoid_and_softplus(-own_u)
    own_slope = -own_sigmoid * own_used
    own_pair = own_softplus * own_used
    own_weight = (own_slope * temp).astype(BF16).astype(F32)
    own_sums = [jnp.sum(value, axis=0, keepdims=True) for value in (own_pair, own_slope, own_slope * (own_u - shift))]
    used = lax.fori_loop(0, counts.shape[0], lambda i, sum: sum + counts[i], 0).astype(F32)

    column_tile = lax.broadcasted_iota(jnp.int32, (8, 512), 1) // T
    columns_used = jnp.zeros((8, 512), F32)
    for k, s in enumerate(ORDER):
        columns_used = jnp.where(
            column_tile == k, tile_used(x if s < 8 else pair_i, ring(y + s), z, core), columns_used
        )

    for entry in GATHER[at_once:]:
        run(*entry)
    for key in tuple(gathered):
        if key[0] == IMG:
            arrive(*key)

    def arrive_texts(c):
        for key in tuple(gathered):
            _, column, piece, k = key
            base = (piece if column == CORE else column) * 8
            early = ORDER.index(base + ring_slot(k, 0)) >= 8
            if key[0] == TXT and early == (c % 2 == 1) and (column == CORE) == (c >= 2):
                arrive(*key)

    def block(c, sums):
        turn = logits.at[c % 2]
        turn[...] = lax.dot_general(
            txt[pl.ds(c * 256, 256), :], img[...], (((1,), (1,)), ((), ())), preferred_element_type=F32
        )
        tc = core if c < 2 else 1 - core
        pair_sum, slope_sum, scaled_sum = sums
        for k in range(8):
            scaled = turn[tile(k), :] * temp
            u = scaled + shift
            slope, pair = sigmoid_and_softplus(u)
            if (c, k) == (1, 7):
                row = lax.broadcasted_iota(jnp.int32, (T, 512), 0)
                column = lax.broadcasted_iota(jnp.int32, (T, 512), 1)
                own = row + 15 * T == column
                slope = jnp.where(own, 0.0, slope)
                pair = jnp.where(own, 0.0, pair)
            slot = ORDER[c % 2 * 8 + k]
            used = tile_used(pair_t if slot >= 8 else x, y, ring(z + slot), tc)
            weight[pl.ds(c * 256 + k * T, T), :] = (slope * (columns_used[:1] * used * temp)).astype(BF16)

            def folded(value):
                return jnp.sum(value.reshape(T // 8, 8, 512), axis=0)

            pair_sum = pair_sum + used * folded(pair)
            slope_sum = slope_sum + used * folded(slope)
            scaled_sum = scaled_sum + used * folded(slope * scaled)
        return pair_sum, slope_sum, scaled_sum

    zero = jnp.zeros((8, 512), F32)
    totals = (zero, zero, zero)
    for c in range(4):
        arrive_texts(c)
    for c in (1, 0, 3, 2):
        totals = block(c, totals)
    pair_sum, slope_sum, scaled_sum = totals

    lane = lax.broadcasted_iota(jnp.int32, (8, 128), 1)

    def own_total():
        whole = [
            jnp.sum(value * columns_used, axis=(0, 1), keepdims=True)
            for value in (pair_sum, slope_sum, scaled_sum)
        ]
        vector = jnp.zeros((8, 128), F32)
        for k in range(3):
            vector = jnp.where(lane == k, whole[k] + own_sums[k], vector)
        return vector

    scal_sent = []

    def scalar_copy(stage, d, mine, slot, peer):
        return pltpu.make_async_remote_copy(
            src_ref=scal.at[stage, mine],
            dst_ref=scal.at[stage, slot],
            send_sem=ssem.at[SCAL + stage * 8 + d],
            recv_sem=rsem.at[SCAL + stage * 8 + slot],
            device_id=peer,
            device_id_type=MESH,
        )

    def spread(stage, mine, peer_of, value):
        scal[stage, mine] = value
        for d in range(1, RING):
            made = scalar_copy(stage, d, mine, mine, peer_of(d))
            made.start()
            scal_sent.append(made)

    def summed(stage, mine, peer_of):
        for d in range(1, RING):
            scalar_copy(stage, d, mine, ring(mine + d), peer_of(d)).wait_recv()
        total = scal[stage, 0]
        for k in range(1, RING):
            total = total + scal[stage, k]
        return total

    def rows_of(group):
        return pl.ds(group * 128, 128)

    def text_dir(first):
        return jnp.dot(weight[first : first + 128, :], img[...], preferred_element_type=F32)

    core_back = {}

    def other_texts(group):
        out_c[rows_of(group), :] = text_dir(512 + group * 128).astype(BF16)
        core_back[group] = send(out_c.at[rows_of(group)], from_c.at[rows_of(group)], core_mate)

    def own_images(group):
        img_sum[rows_of(group), :] = lax.dot_general(
            weight[:, group * 128 : group * 128 + 128], txt[...], (((0,), (0,)), ((), ())), preferred_element_type=F32
        )

    def own_texts(group):
        txt_sum[rows_of(group), :] = text_dir(group * 128)

    computed = set()

    def compute(ring, group):
        if (ring, group) in computed:
            return
        computed.add((ring, group))
        if ring == IMG:
            own_images(group)
        else:
            own_texts(group)
            if group < 3:
                other_texts(group + 1)

    core_seen = set()

    def own_part(ring, slot, part):
        group = ORDER.index(slot) // 4
        compute(ring, group)
        if ring == IMG:
            return img_sum[at(slot, part), :]
        if group not in core_seen:
            core_seen.add(group)
            core_back[group].wait_recv()
        return txt_sum[at(slot, part), :] + from_c[at(slot, part), :].astype(F32)

    out, back = (txt_out, img_out), (txt_back, img_back)
    coming, places = {}, {}

    def landing(column, piece, k, way):
        row = places.setdefault((column, piece, k, way), len(places) * 16)
        return pl.ds(row, 16)

    def received(ring, column, piece, k, way):
        key = (ring, column, piece, k, way)
        if coming[key] is not None:
            coming[key].wait_recv()
            coming[key] = None
        return back[ring][landing(column, piece, k, way), :].astype(F32)

    def partial(ring, column, piece, k, way):
        value = own_part(ring, column * 8 + ring_slot(k, way), PIECES[piece])
        if column == OWN and ROUTES[piece][MATE][k] is None:
            value = value + received(ring, MATE, piece, k, way)
        for further, parent in ROUTES[piece][column].items():
            if parent != k:
                continue
            if further < 4:
                for w in (0, 1) if k == 0 else (way,):
                    value = value + received(ring, column, piece, further, w)
            else:
                extra = received(ring, column, piece, 4, 0)
                value = value + (extra if k == 0 else jnp.where(odd == way, extra, 0.0))
        return value

    def pass_back(ring, column, piece, k):
        parent, part = ROUTES[piece][column][k], PIECES[piece]
        for way in ways(k):
            slot = column * 8 + ring_slot(k, way)
            out[ring][at(slot, part), :] = partial(ring, column, piece, k, way).astype(BF16)
            if parent is None:
                peer = ring_mate[ring]
            elif k < 4:
                peer = ring_peer[ring]((parent - k) * (1 - 2 * way))
            else:
                peer = ring_peer[ring](jnp.where(odd == 1, k - parent, parent - k))
            target = back[ring].at[landing(column, piece, k, way)]
            coming[ring, column, piece, k, way] = send(out[ring].at[at(slot, part)], target, peer)

    ahead = 0
    other_texts(0)
    for n in range(len(REDUCE) + ahead):
        if n < len(REDUCE):
            pass_back(IMG, *REDUCE[n])
        if n >= ahead:
            pass_back(TXT, *REDUCE[n - ahead])
        if n == 3:
            spread(0, y, y_peer, own_total())
        elif n == 10:
            spread(1, z, z_peer, summed(0, y, y_peer))
        elif n == 15:
            spread(2, my_xc, xc_peer, summed(1, z, z_peer))

    total = summed(2, my_xc, xc_peer)
    means = total / used
    scalars[...] = means

    ends = ((txt_unit, txt_length, img_wide, grad_txt), (img_unit, img_length, txt_wide, grad_img))
    for n in (TXT, IMG):
        unit, length, other, grad = ends[n]
        top, low = (partial(n, OWN, piece, 0, 0) for piece in (0, 1))
        total_dir = jnp.concatenate([top, low], axis=0) + own_weight * other
        grad[...] = projected(total_dir, unit, length)

    assert len(sent) <= SCAL and len(places) * 16 <= back[0].shape[0]
    for made in sent + scal_sent:
        made.wait_send()


def place_results(scalars, grad_img, grad_txt, loss, grad_log_temp, grad_bias, img_out, txt_out, staged, arrived):
    moved = [
        pltpu.make_async_copy(source, target, arrived.at[k])
        for k, (source, target) in enumerate(
            (
                (grad_img, img_out),
                (grad_txt, txt_out),
                (staged.at[0], loss),
                (staged.at[1], grad_bias),
                (staged.at[2], grad_log_temp),
            )
        )
    ]
    for made in moved[:2]:
        made.start()
    for k in range(3):
        staged[k, 0] = scalars[0, k]
        moved[2 + k].start()
    for made in moved:
        made.wait()


def body(images, texts, row_counts, log_temp, bias):
    rows, width = images.shape
    scalar = jax.ShapeDtypeStruct((1,), F32)
    grad = jax.ShapeDtypeStruct((rows, width), F32)
    vmem = pl.BlockSpec(memory_space=pltpu.VMEM)
    found = pl.pallas_call(
        kernel,
        out_shape=(jax.ShapeDtypeStruct((8, 128), F32), grad, grad),
        in_specs=[pl.BlockSpec(memory_space=pltpu.HBM)] * 5,
        out_specs=(vmem, vmem, vmem),
        scratch_shapes=[
            pltpu.VMEM((T, width), BF16),
            pltpu.VMEM((T, width), BF16),
            pltpu.SMEM(row_counts.shape, jnp.int32),
            pltpu.SMEM((1,), F32),
            pltpu.SMEM((1,), F32),
            pltpu.VMEM((512, width), BF16),
            pltpu.VMEM((1024, width), BF16),
            pltpu.VMEM((1024, 512), BF16),
            pltpu.VMEM((2, 256, 512), F32),
            pltpu.VMEM((512, width), BF16),
            pltpu.VMEM((512, width), BF16),
            pltpu.VMEM((512, width), F32),
            pltpu.VMEM((512, width), F32),
            pltpu.VMEM((512, width), BF16),
            pltpu.VMEM((512, width), BF16),
            pltpu.VMEM((480, width), BF16),
            pltpu.VMEM((480, width), BF16),
            pltpu.VMEM((3, 8, 8, 128), F32),
            pltpu.SemaphoreType.DMA((5,)),
            pltpu.SemaphoreType.DMA((N_SEM,)),
            pltpu.SemaphoreType.DMA((N_SEM,)),
        ],
        compiler_params=pltpu.CompilerParams(
            collective_id=0, has_side_effects=True, vmem_limit_bytes=60 << 20
        ),
        cost_estimate=pl.CostEstimate(flops=6 * 512 * 1024 * width, bytes_accessed=4 << 20, transcendentals=1 << 20),
    )(images, texts, row_counts, log_temp, bias)
    return pl.pallas_call(
        place_results,
        out_shape=(scalar, scalar, scalar, grad, grad),
        in_specs=[vmem] * 3,
        out_specs=[pl.BlockSpec(memory_space=pltpu.HBM)] * 5,
        scratch_shapes=[pltpu.SMEM((3, 1), F32), pltpu.SemaphoreType.DMA((5,))],
    )(*found)


def solution(mesh):
    return jax.shard_map(
        body,
        mesh=mesh,
        in_specs=(P(("blk", "sub"), None), P(("blk", "sub"), None), P(), P(), P()),
        out_specs=(P(), P(), P(), P(("blk", "sub"), None), P(("blk", "sub"), None)),
        check_vma=False,
    )
```

```python
import functools

import jax
import jax.numpy as jnp
from jax import lax
from jax.experimental import pallas as pl
from jax.experimental.pallas import tpu as pltpu
from jax.sharding import PartitionSpec as P

MESH = pl.DeviceIdType.MESH
F32 = jnp.float32
BF16 = jnp.bfloat16
T = 32
RING = 8
PIECES_OUT, CORE_OUT, PIECES_BACK, CORE_BACK, SCALARS_OUT, N_SENT = range(6)
N_RECEIVED = 89
FULL = (0, T)
PIECES = ((0, 16), (16, 16))
OWN, MATE = 0, 1
ROUTES = (
    ({1: 0, 2: 0, 3: 2, 4: 3}, {0: None, 1: None, 2: None, 3: None, 4: 2}),
    ({1: 0, 2: 1, 3: 2, 4: 2}, {0: None, 1: 0, 2: None, 3: 1, 4: 3}),
)
CORE = 2
GATHER = (
    (MATE, 1, 0), (OWN, 1, 1), (OWN, 0, 2), (OWN, 0, 1), (MATE, 0, 0), (CORE, OWN, 0), (MATE, 1, 1), (CORE, MATE, 0),
    (OWN, 1, 2), (MATE, 0, 1), (OWN, 0, 3), (MATE, 0, 2), (CORE, OWN, 1), (MATE, 1, 3), (OWN, 1, 3), (OWN, 1, 4),
    (MATE, 1, 2), (CORE, OWN, 2), (MATE, 0, 3), (OWN, 0, 4), (CORE, MATE, 1), (MATE, 0, 4), (MATE, 1, 4),
    (CORE, OWN, 3), (CORE, MATE, 2), (CORE, OWN, 4), (CORE, MATE, 3), (CORE, MATE, 4),
)
REDUCE = (
    (MATE, 0, 4), (MATE, 1, 4), (MATE, 0, 3), (OWN, 0, 4), (MATE, 1, 2), (OWN, 1, 3), (OWN, 1, 4), (MATE, 1, 3),
    (MATE, 0, 2), (MATE, 0, 1), (OWN, 0, 3), (OWN, 1, 2), (MATE, 1, 1), (OWN, 0, 2), (OWN, 0, 1), (OWN, 1, 1),
    (MATE, 1, 0), (MATE, 0, 0),
)
ORDER = (12, 11, 13, 4, 10, 14, 5, 3, 9, 15, 6, 2, 7, 1, 8, 0)


def ways(k):
    return (0, 1) if 0 < k < 4 else (0,)


def ring_slot(k, way):
    return (RING - k) % RING if way == 0 else k


def place():
    blk, sub = lax.axis_index("blk"), lax.axis_index("sub")
    core = lax.rem(blk, 2)
    y = lax.rem(lax.div(blk, 2), RING)
    z = lax.rem(lax.div(blk, 16), 2) * 4 + sub
    x = lax.div(blk, 32)
    return x, y, z, core


def member(x, y, z, core):
    return ((x * 2 + lax.div(z, 4)) * RING + y) * 2 + core


def device(x, y, z, core):
    return (member(x, y, z, core), lax.rem(z, 4))


def ring(value):
    return lax.rem(value, RING)


def normalized(values):
    wide = values.astype(F32)
    length = jnp.sqrt(jnp.sum(wide * wide, axis=1, keepdims=True) + 1e-06)
    return wide / length, length


def projected(grad, unit, length):
    return (grad - unit * jnp.sum(unit * grad, axis=1, keepdims=True)) / length


def sigmoid_and_softplus(u):
    small = jnp.exp(-jnp.abs(u))
    ratio = 1.0 / (1.0 + small)
    sigmoid = jnp.where(u >= 0.0, ratio, small * ratio)
    softplus = jnp.maximum(u, 0.0) + jnp.log1p(small)
    return sigmoid, softplus


def at(slot, part=FULL):
    return pl.ds((slot // 16 * 16 + ORDER.index(slot % 16)) * T + part[0], part[1])


def tile(slot):
    return pl.ds(slot * T, T)


def kernel(
    img_hbm, txt_hbm, counts_hbm, log_temp_hbm, bias_hbm,
    scalars, grad_img, grad_txt,
    img_in, txt_in, counts, log_temp, bias, img, txt, weight, logits,
    out_c, from_c, img_sum, txt_sum, img_out, txt_out, img_back, txt_back, scal, local, ssem, rsem,
):
    x, y, z, core = place()
    pair_i = x + 1 - 2 * lax.rem(x, 2)
    pair_t = lax.rem(x + 3 + 2 * lax.rem(x, 2), 4)

    def y_peer(d):
        return device(x, ring(y + RING + d), z, core)

    def z_peer(d):
        return device(x, y, ring(z + RING + d), core)

    my_xc = x * 2 + core

    def xc_peer(d):
        other = ring(my_xc + d)
        return device(lax.div(other, 2), y, z, lax.rem(other, 2))

    img_mate = device(pair_i, y, z, core)
    txt_mate = device(pair_t, y, z, core)
    core_mate = device(x, y, z, 1 - core)

    fetched = [
        pltpu.make_async_copy(source, target, local.at[k])
        for k, (source, target) in enumerate(
            ((txt_hbm, txt_in), (img_hbm, img_in), (counts_hbm, counts), (log_temp_hbm, log_temp), (bias_hbm, bias))
        )
    ]
    for made in fetched:
        made.start()

    barrier = pltpu.get_barrier_semaphore()
    for d in range(1, RING):
        for peer in (y_peer(d), z_peer(d), xc_peer(d)):
            pl.semaphore_signal(barrier, inc=1, device_id=peer, device_id_type=MESH)

    def tile_used(x, y, z, core):
        return jnp.where(counts[member(x, y, z, core)] > T * lax.rem(z, 4), 1.0, 0.0)

    fetched[0].wait()
    txt_unit, txt_length = normalized(txt_in[...])
    txt_half = txt_unit.astype(BF16)
    txt[at(0), :] = txt_half

    rows_sent = [0] * N_SENT
    used_sems = []

    def fresh():
        used_sems.append(len(used_sems))
        return used_sems[-1]

    def remote(src, dst, outgoing, index, peer):
        return pltpu.make_async_remote_copy(
            src_ref=src,
            dst_ref=dst,
            send_sem=ssem.at[outgoing],
            recv_sem=rsem.at[index],
            device_id=peer,
            device_id_type=MESH,
        )

    def send(src, dst, peer, outgoing, index):
        remote(src, dst, outgoing, index, peer).start()
        rows_sent[outgoing] += src.shape[0]

    def any_rows(rows):
        return txt.at[pl.ds(0, rows)]

    def wait_for(index, rows):
        remote(any_rows(rows), any_rows(rows), 0, index, core_mate).wait_recv()

    odd = lax.rem(core, 2)
    TXT, IMG = 0, 1
    ring_buf, ring_peer, ring_mate = (txt, img), (z_peer, y_peer), (txt_mate, img_mate)

    pl.semaphore_wait(barrier, 3 * (RING - 1))

    gathered = {}

    def way_on(ring, k, parent):
        return ring_peer[ring](jnp.where(odd == 1, parent - k, k - parent))

    def move(ring, column, piece, k):
        buf, part = ring_buf[ring], PIECES[piece]
        parent, index = ROUTES[piece][column][k], fresh()
        for way in ways(k):
            slot = ring_slot(k, way)
            if parent is None:
                source, target, peer = at(slot, part), at(8 + slot, part), ring_mate[ring]
            elif k < 4:
                source, target = at(column * 8 + ring_slot(parent, way), part), at(column * 8 + slot, part)
                peer = ring_peer[ring]((k - parent) * (1 - 2 * way))
            else:
                up, down = (ORDER.index(column * 8 + ring_slot(parent, w)) for w in (0, 1))
                first = jnp.where(odd == 1, down, up) * T + part[0]
                source, target = pl.ds(pl.multiple_of(first, 16), 16), at(column * 8 + slot, part)
                peer = way_on(ring, k, parent)
            send(buf.at[source], buf.at[target], peer, PIECES_OUT, index)
        gathered[ring, column, piece, k] = (index, part[1] * len(ways(k)))

    def arrive(*key):
        if gathered[key] is not None:
            wait_for(*gathered[key])
            gathered[key] = None

    def run(column, piece, k, rings=(0, 1)):
        if column == CORE:
            if TXT not in rings:
                return
            base = piece * 8
            if k or base:
                for n in range(2):
                    arrive(TXT, piece, n, k)
            index = fresh()
            for way in ways(k):
                slot = base + ring_slot(k, way)
                send(txt.at[at(slot)], txt.at[at(16 + slot)], core_mate, CORE_OUT, index)
            gathered[TXT, CORE, piece, k] = (index, T * len(ways(k)))
            return
        parent = ROUTES[piece][column][k]
        for n in rings:
            if parent is None and k:
                arrive(n, OWN, piece, k)
            elif parent is not None and (parent or column == MATE):
                arrive(n, column, piece, parent)
            move(n, column, piece, k)

    at_once = 6
    for entry in GATHER[:at_once]:
        run(*entry, rings=(TXT,))
    fetched[1].wait()
    img_unit, img_length = normalized(img_in[...])
    img_half = img_unit.astype(BF16)
    img[at(0), :] = img_half
    for entry in GATHER[:at_once]:
        run(*entry, rings=(IMG,))
    for made in fetched[2:]:
        made.wait()
    own_used = tile_used(x, y, z, core)
    temp = jnp.exp(jnp.full((1, 1), log_temp[0], F32))
    shift = bias[0]

    img_wide, txt_wide = img_half.astype(F32), txt_half.astype(F32)
    own_u = temp * jnp.sum(img_wide * txt_wide, axis=1, keepdims=True) + shift
    own_sigmoid, own_softplus = sigmoid_and_softplus(-own_u)
    own_slope = -own_sigmoid * own_used
    own_pair = own_softplus * own_used
    own_weight = (own_slope * temp).astype(BF16).astype(F32)
    own_sums = [jnp.sum(value, axis=0, keepdims=True) for value in (own_pair, own_slope, own_slope * (own_u - shift))]
    used = lax.fori_loop(0, counts.shape[0], lambda i, sum: sum + counts[i], 0).astype(F32)

    column_tile = lax.broadcasted_iota(jnp.int32, (8, 512), 1) // T
    columns_used = jnp.zeros((8, 512), F32)
    for k, s in enumerate(ORDER):
        columns_used = jnp.where(
            column_tile == k, tile_used(x if s < 8 else pair_i, ring(y + s), z, core), columns_used
        )

    for entry in GATHER[at_once:]:
        run(*entry)
    for key in tuple(gathered):
        if key[0] == IMG:
            arrive(*key)

    def arrive_texts(c):
        for key in tuple(gathered):
            _, column, piece, k = key
            base = (piece if column == CORE else column) * 8
            early = ORDER.index(base + ring_slot(k, 0)) >= 8
            if key[0] == TXT and early == (c % 2 == 1) and (column == CORE) == (c >= 2):
                arrive(*key)

    def block(c, sums):
        turn = logits.at[c % 2]
        turn[...] = lax.dot_general(
            txt[pl.ds(c * 256, 256), :], img[...], (((1,), (1,)), ((), ())), preferred_element_type=F32
        )
        tc = core if c < 2 else 1 - core
        pair_sum, slope_sum, scaled_sum = sums
        for k in range(8):
            scaled = turn[tile(k), :] * temp
            u = scaled + shift
            slope, pair = sigmoid_and_softplus(u)
            if (c, k) == (1, 7):
                row = lax.broadcasted_iota(jnp.int32, (T, 512), 0)
                column = lax.broadcasted_iota(jnp.int32, (T, 512), 1)
                own = row + 15 * T == column
                slope = jnp.where(own, 0.0, slope)
                pair = jnp.where(own, 0.0, pair)
            slot = ORDER[c % 2 * 8 + k]
            used = tile_used(pair_t if slot >= 8 else x, y, ring(z + slot), tc)
            weight[pl.ds(c * 256 + k * T, T), :] = (slope * (columns_used[:1] * used * temp)).astype(BF16)

            def folded(value):
                return jnp.sum(value.reshape(T // 8, 8, 512), axis=0)

            pair_sum = pair_sum + used * folded(pair)
            slope_sum = slope_sum + used * folded(slope)
            scaled_sum = scaled_sum + used * folded(slope * scaled)
        return pair_sum, slope_sum, scaled_sum

    def rows_of(group):
        return pl.ds(group * 128, 128)

    def text_dir(first):
        return jnp.dot(weight[first : first + 128, :], img[...], preferred_element_type=F32)

    core_back = {}

    def other_texts(group):
        out_c[rows_of(group), :] = text_dir(512 + group * 128).astype(BF16)
        core_back[group] = fresh()
        send(out_c.at[rows_of(group)], from_c.at[rows_of(group)], core_mate, CORE_BACK, core_back[group])

    zero = jnp.zeros((8, 512), F32)
    totals = (zero, zero, zero)
    for c in range(4):
        arrive_texts(c)
    for c in (3, 2, 1, 0):
        totals = block(c, totals)
        if c == 2:
            other_texts(0)
    pair_sum, slope_sum, scaled_sum = totals

    lane = lax.broadcasted_iota(jnp.int32, (8, 128), 1)

    def own_total():
        whole = [
            jnp.sum(value * columns_used, axis=(0, 1), keepdims=True)
            for value in (pair_sum, slope_sum, scaled_sum)
        ]
        vector = jnp.zeros((8, 128), F32)
        for k in range(3):
            vector = jnp.where(lane == k, whole[k] + own_sums[k], vector)
        return vector

    stage_sems = [fresh() for _ in range(3)]

    def spread(stage, mine, peer_of, value):
        place = scal.at[stage * 8 + mine]
        place[...] = value
        for d in range(1, RING):
            remote(place, place, SCALARS_OUT, stage_sems[stage], peer_of(d)).start()

    def summed(stage):
        others = scal.at[pl.ds(0, RING - 1)]
        remote(others, others, SCALARS_OUT, stage_sems[stage], core_mate).wait_recv()
        total = scal[stage * 8]
        for k in range(1, RING):
            total = total + scal[stage * 8 + k]
        return total

    def own_images(group):
        img_sum[rows_of(group), :] = lax.dot_general(
            weight[:, group * 128 : group * 128 + 128], txt[...], (((0,), (0,)), ((), ())), preferred_element_type=F32
        )

    def own_texts(group):
        txt_sum[rows_of(group), :] = text_dir(group * 128)

    computed = set()

    def compute(ring, group):
        if (ring, group) in computed:
            return
        computed.add((ring, group))
        if ring == IMG:
            own_images(group)
        else:
            own_texts(group)
            if group < 3:
                other_texts(group + 1)

    core_seen = set()

    def own_part(ring, slot, part):
        group = ORDER.index(slot) // 4
        compute(ring, group)
        if ring == IMG:
            return img_sum[at(slot, part), :]
        if group not in core_seen:
            core_seen.add(group)
            wait_for(core_back[group], 128)
        return txt_sum[at(slot, part), :] + from_c[at(slot, part), :].astype(F32)

    out, back = (txt_out, img_out), (txt_back, img_back)
    coming, places = {}, {}

    def landing(column, piece, k, way):
        row = places.setdefault((column, piece, k, way), len(places) * 16)
        return pl.ds(row, 16)

    def received(ring, column, piece, k, way):
        key = (ring, column, piece, k)
        if coming[key] is not None:
            wait_for(*coming[key])
            coming[key] = None
        return back[ring][landing(column, piece, k, way), :].astype(F32)

    def partial(ring, column, piece, k, way):
        value = own_part(ring, column * 8 + ring_slot(k, way), PIECES[piece])
        if column == OWN and ROUTES[piece][MATE][k] is None:
            value = value + received(ring, MATE, piece, k, way)
        for further, parent in ROUTES[piece][column].items():
            if parent != k:
                continue
            if further < 4:
                for w in (0, 1) if k == 0 else (way,):
                    value = value + received(ring, column, piece, further, w)
            else:
                extra = received(ring, column, piece, 4, 0)
                value = value + (extra if k == 0 else jnp.where(odd == way, extra, 0.0))
        return value

    def pass_back(ring, column, piece, k):
        parent, part, index = ROUTES[piece][column][k], PIECES[piece], fresh()
        for way in ways(k):
            slot = column * 8 + ring_slot(k, way)
            out[ring][at(slot, part), :] = partial(ring, column, piece, k, way).astype(BF16)
            if parent is None:
                peer = ring_mate[ring]
            elif k < 4:
                peer = ring_peer[ring]((parent - k) * (1 - 2 * way))
            else:
                peer = ring_peer[ring](jnp.where(odd == 1, k - parent, parent - k))
            target = back[ring].at[landing(column, piece, k, way)]
            send(out[ring].at[at(slot, part)], target, peer, PIECES_BACK, index)
        coming[ring, column, piece, k] = (index, part[1] * len(ways(k)))

    ahead = 0
    for n in range(len(REDUCE) + ahead):
        if n < len(REDUCE):
            pass_back(IMG, *REDUCE[n])
        if n >= ahead:
            pass_back(TXT, *REDUCE[n - ahead])
        if n == 3:
            spread(0, y, y_peer, own_total())
        elif n == 10:
            spread(1, z, z_peer, summed(0))
        elif n == 15:
            spread(2, my_xc, xc_peer, summed(1))

    total = summed(2)
    means = total / used
    scalars[...] = means

    ends = ((txt_unit, txt_length, img_wide, grad_txt), (img_unit, img_length, txt_wide, grad_img))
    for n in (TXT, IMG):
        unit, length, other, grad = ends[n]
        top, low = (partial(n, OWN, piece, 0, 0) for piece in (0, 1))
        total_dir = jnp.concatenate([top, low], axis=0) + own_weight * other
        grad[...] = projected(total_dir, unit, length)

    assert len(used_sems) == N_RECEIVED and len(places) * 16 <= back[0].shape[0]
    for kind, rows in enumerate(rows_sent):
        if rows:
            remote(any_rows(rows), any_rows(rows), kind, 0, core_mate).wait_send()
    scalars_sent = scal.at[pl.ds(0, 3 * (RING - 1))]
    remote(scalars_sent, scalars_sent, SCALARS_OUT, 0, core_mate).wait_send()


def place_results(scalars, grad_img, grad_txt, loss, grad_log_temp, grad_bias, img_out, txt_out, staged, arrived):
    moved = [
        pltpu.make_async_copy(source, target, arrived.at[k])
        for k, (source, target) in enumerate(
            (
                (grad_img, img_out),
                (grad_txt, txt_out),
                (staged.at[0], loss),
                (staged.at[1], grad_bias),
                (staged.at[2], grad_log_temp),
            )
        )
    ]
    for made in moved[:2]:
        made.start()
    for k in range(3):
        staged[k, 0] = scalars[0, k]
        moved[2 + k].start()
    for made in moved:
        made.wait()


def body(images, texts, row_counts, log_temp, bias):
    rows, width = images.shape
    scalar = jax.ShapeDtypeStruct((1,), F32)
    grad = jax.ShapeDtypeStruct((rows, width), F32)
    vmem = pl.BlockSpec(memory_space=pltpu.VMEM)
    found = pl.pallas_call(
        kernel,
        out_shape=(jax.ShapeDtypeStruct((8, 128), F32), grad, grad),
        in_specs=[pl.BlockSpec(memory_space=pltpu.HBM)] * 5,
        out_specs=(vmem, vmem, vmem),
        scratch_shapes=[
            pltpu.VMEM((T, width), BF16),
            pltpu.VMEM((T, width), BF16),
            pltpu.SMEM(row_counts.shape, jnp.int32),
            pltpu.SMEM((1,), F32),
            pltpu.SMEM((1,), F32),
            pltpu.VMEM((512, width), BF16),
            pltpu.VMEM((1024, width), BF16),
            pltpu.VMEM((1024, 512), BF16),
            pltpu.VMEM((2, 256, 512), F32),
            pltpu.VMEM((512, width), BF16),
            pltpu.VMEM((512, width), BF16),
            pltpu.VMEM((512, width), F32),
            pltpu.VMEM((512, width), F32),
            pltpu.VMEM((512, width), BF16),
            pltpu.VMEM((512, width), BF16),
            pltpu.VMEM((480, width), BF16),
            pltpu.VMEM((480, width), BF16),
            pltpu.VMEM((24, 8, 128), F32),
            pltpu.SemaphoreType.DMA((5,)),
            pltpu.SemaphoreType.DMA((N_SENT,)),
            pltpu.SemaphoreType.DMA((N_RECEIVED,)),
        ],
        compiler_params=pltpu.CompilerParams(
            collective_id=0, has_side_effects=True, vmem_limit_bytes=60 << 20
        ),
        cost_estimate=pl.CostEstimate(flops=6 * 512 * 1024 * width, bytes_accessed=4 << 20, transcendentals=1 << 20),
    )(images, texts, row_counts, log_temp, bias)
    return pl.pallas_call(
        place_results,
        out_shape=(scalar, scalar, scalar, grad, grad),
        in_specs=[vmem] * 3,
        out_specs=[pl.BlockSpec(memory_space=pltpu.HBM)] * 5,
        scratch_shapes=[pltpu.SMEM((3, 1), F32), pltpu.SemaphoreType.DMA((5,))],
    )(*found)


def solution(mesh):
    return jax.shard_map(
        body,
        mesh=mesh,
        in_specs=(P(("blk", "sub"), None), P(("blk", "sub"), None), P(), P(), P()),
        out_specs=(P(), P(), P(), P(("blk", "sub"), None), P(("blk", "sub"), None)),
        check_vma=False,
    )
```

```python
import functools

import jax
import jax.numpy as jnp
from jax import lax
from jax.experimental import pallas as pl
from jax.experimental.pallas import tpu as pltpu
from jax.sharding import PartitionSpec as P

MESH = pl.DeviceIdType.MESH
F32 = jnp.float32
BF16 = jnp.bfloat16
T = 32
RING = 8
PIECES_OUT, CORE_OUT, PIECES_BACK, CORE_BACK, SCALARS_OUT, N_SENT = range(6)
N_RECEIVED = 89
FULL = (0, T)
PIECES = ((0, 16), (16, 16))
OWN, MATE = 0, 1
ROUTES = (
    ({1: 0, 2: 0, 3: 2, 4: 3}, {0: None, 1: None, 2: None, 3: None, 4: 2}),
    ({1: 0, 2: 1, 3: 2, 4: 2}, {0: None, 1: 0, 2: None, 3: 1, 4: 3}),
)
CORE = 2
GATHER = (
    (MATE, 1, 0), (OWN, 1, 1), (OWN, 0, 2), (OWN, 0, 1), (MATE, 0, 0), (CORE, OWN, 0), (MATE, 1, 1), (CORE, MATE, 0),
    (OWN, 1, 2), (MATE, 0, 1), (OWN, 0, 3), (MATE, 0, 2), (CORE, OWN, 1), (MATE, 1, 3), (OWN, 1, 3), (OWN, 1, 4),
    (MATE, 1, 2), (CORE, OWN, 2), (MATE, 0, 3), (OWN, 0, 4), (CORE, MATE, 1), (MATE, 0, 4), (MATE, 1, 4),
    (CORE, OWN, 3), (CORE, MATE, 2), (CORE, OWN, 4), (CORE, MATE, 3), (CORE, MATE, 4),
)
REDUCE = (
    (MATE, 0, 4), (MATE, 1, 4), (MATE, 0, 3), (OWN, 0, 4), (MATE, 1, 2), (OWN, 1, 3), (OWN, 1, 4), (MATE, 1, 3),
    (MATE, 0, 2), (MATE, 0, 1), (OWN, 0, 3), (OWN, 1, 2), (MATE, 1, 1), (OWN, 0, 2), (OWN, 0, 1), (OWN, 1, 1),
    (MATE, 1, 0), (MATE, 0, 0),
)
ORDER = (12, 11, 13, 4, 10, 14, 5, 3, 9, 15, 6, 2, 7, 1, 8, 0)


def ways(k):
    return (0, 1) if 0 < k < 4 else (0,)


def ring_slot(k, way):
    return (RING - k) % RING if way == 0 else k


def place():
    blk, sub = lax.axis_index("blk"), lax.axis_index("sub")
    core = lax.rem(blk, 2)
    y = lax.rem(lax.div(blk, 2), RING)
    z = lax.rem(lax.div(blk, 16), 2) * 4 + sub
    x = lax.div(blk, 32)
    return x, y, z, core


def member(x, y, z, core):
    return ((x * 2 + lax.div(z, 4)) * RING + y) * 2 + core


def device(x, y, z, core):
    return (member(x, y, z, core), lax.rem(z, 4))


def ring(value):
    return lax.rem(value, RING)


def normalized(values):
    wide = values.astype(F32)
    length = jnp.sqrt(jnp.sum(wide * wide, axis=1, keepdims=True) + 1e-06)
    return wide / length, length


def projected(grad, unit, length):
    return (grad - unit * jnp.sum(unit * grad, axis=1, keepdims=True)) / length


def sigmoid_and_softplus(u):
    small = jnp.exp(-jnp.abs(u))
    ratio = 1.0 / (1.0 + small)
    sigmoid = jnp.where(u >= 0.0, ratio, small * ratio)
    softplus = jnp.maximum(u, 0.0) + jnp.log1p(small)
    return sigmoid, softplus


def at(slot, part=FULL):
    return pl.ds((slot // 16 * 16 + ORDER.index(slot % 16)) * T + part[0], part[1])


def tile(slot):
    return pl.ds(slot * T, T)


def kernel(
    img_hbm, txt_hbm, counts_hbm, log_temp_hbm, bias_hbm,
    scalars, grad_img, grad_txt,
    img_in, txt_in, counts, log_temp, bias, img, txt, weight, logits,
    out_c, from_c, img_sum, txt_sum, img_out, txt_out, img_back, txt_back, scal, local, ssem, rsem,
):
    x, y, z, core = place()
    pair_i = x + 1 - 2 * lax.rem(x, 2)
    pair_t = lax.rem(x + 3 + 2 * lax.rem(x, 2), 4)

    def y_peer(d):
        return device(x, ring(y + RING + d), z, core)

    def z_peer(d):
        return device(x, y, ring(z + RING + d), core)

    my_xc = x * 2 + core

    def xc_peer(d):
        other = ring(my_xc + d)
        return device(lax.div(other, 2), y, z, lax.rem(other, 2))

    img_mate = device(pair_i, y, z, core)
    txt_mate = device(pair_t, y, z, core)
    core_mate = device(x, y, z, 1 - core)

    fetched = [
        pltpu.make_async_copy(source, target, local.at[k])
        for k, (source, target) in enumerate(
            ((txt_hbm, txt_in), (img_hbm, img_in), (counts_hbm, counts), (log_temp_hbm, log_temp), (bias_hbm, bias))
        )
    ]
    for made in fetched:
        made.start()

    barrier = pltpu.get_barrier_semaphore()
    for d in range(1, RING):
        for peer in (y_peer(d), z_peer(d), xc_peer(d)):
            pl.semaphore_signal(barrier, inc=1, device_id=peer, device_id_type=MESH)

    def tile_used(x, y, z, core):
        return jnp.where(counts[member(x, y, z, core)] > T * lax.rem(z, 4), 1.0, 0.0)

    fetched[0].wait()
    txt_unit, txt_length = normalized(txt_in[...])
    txt_half = txt_unit.astype(BF16)
    txt[at(0), :] = txt_half

    rows_sent = [0] * N_SENT
    used_sems = []

    def fresh():
        used_sems.append(len(used_sems))
        return used_sems[-1]

    def remote(src, dst, outgoing, index, peer):
        return pltpu.make_async_remote_copy(
            src_ref=src,
            dst_ref=dst,
            send_sem=ssem.at[outgoing],
            recv_sem=rsem.at[index],
            device_id=peer,
            device_id_type=MESH,
        )

    def send(src, dst, peer, outgoing, index):
        remote(src, dst, outgoing, index, peer).start()
        rows_sent[outgoing] += src.shape[0]

    def any_rows(rows):
        return txt.at[pl.ds(0, rows)]

    def wait_for(index, rows):
        remote(any_rows(rows), any_rows(rows), 0, index, core_mate).wait_recv()

    odd = lax.rem(core, 2)
    TXT, IMG = 0, 1
    ring_buf, ring_peer, ring_mate = (txt, img), (z_peer, y_peer), (txt_mate, img_mate)

    pl.semaphore_wait(barrier, 3 * (RING - 1))

    gathered = {}

    def way_on(ring, k, parent):
        return ring_peer[ring](jnp.where(odd == 1, parent - k, k - parent))

    def move(ring, column, piece, k):
        buf, part = ring_buf[ring], PIECES[piece]
        parent, index = ROUTES[piece][column][k], fresh()
        for way in ways(k):
            slot = ring_slot(k, way)
            if parent is None:
                source, target, peer = at(slot, part), at(8 + slot, part), ring_mate[ring]
            elif k < 4:
                source, target = at(column * 8 + ring_slot(parent, way), part), at(column * 8 + slot, part)
                peer = ring_peer[ring]((k - parent) * (1 - 2 * way))
            else:
                up, down = (ORDER.index(column * 8 + ring_slot(parent, w)) for w in (0, 1))
                first = jnp.where(odd == 1, down, up) * T + part[0]
                source, target = pl.ds(pl.multiple_of(first, 16), 16), at(column * 8 + slot, part)
                peer = way_on(ring, k, parent)
            send(buf.at[source], buf.at[target], peer, PIECES_OUT, index)
        gathered[ring, column, piece, k] = (index, part[1] * len(ways(k)))

    def arrive(*key):
        if gathered[key] is not None:
            wait_for(*gathered[key])
            gathered[key] = None

    def run(column, piece, k, rings=(0, 1)):
        if column == CORE:
            if TXT not in rings:
                return
            base = piece * 8
            if k or base:
                for n in range(2):
                    arrive(TXT, piece, n, k)
            index = fresh()
            for way in ways(k):
                slot = base + ring_slot(k, way)
                send(txt.at[at(slot)], txt.at[at(16 + slot)], core_mate, CORE_OUT, index)
            gathered[TXT, CORE, piece, k] = (index, T * len(ways(k)))
            return
        parent = ROUTES[piece][column][k]
        for n in rings:
            if parent is None and k:
                arrive(n, OWN, piece, k)
            elif parent is not None and (parent or column == MATE):
                arrive(n, column, piece, parent)
            move(n, column, piece, k)

    at_once = 6
    for entry in GATHER[:at_once]:
        run(*entry, rings=(TXT,))
    fetched[1].wait()
    img_unit, img_length = normalized(img_in[...])
    img_half = img_unit.astype(BF16)
    img[at(0), :] = img_half
    for entry in GATHER[:at_once]:
        run(*entry, rings=(IMG,))
    for made in fetched[2:]:
        made.wait()
    own_used = tile_used(x, y, z, core)
    temp = jnp.exp(jnp.full((1, 1), log_temp[0], F32))
    shift = bias[0]

    img_wide, txt_wide = img_half.astype(F32), txt_half.astype(F32)
    own_u = temp * jnp.sum(img_wide * txt_wide, axis=1, keepdims=True) + shift
    own_sigmoid, own_softplus = sigmoid_and_softplus(-own_u)
    own_slope = -own_sigmoid * own_used
    own_pair = own_softplus * own_used
    own_weight = (own_slope * temp).astype(BF16).astype(F32)
    own_sums = [jnp.sum(value, axis=0, keepdims=True) for value in (own_pair, own_slope, own_slope * (own_u - shift))]
    used = lax.fori_loop(0, counts.shape[0], lambda i, sum: sum + counts[i], 0).astype(F32)

    column_tile = lax.broadcasted_iota(jnp.int32, (8, 512), 1) // T
    columns_used = jnp.zeros((8, 512), F32)
    for k, s in enumerate(ORDER):
        columns_used = jnp.where(
            column_tile == k, tile_used(x if s < 8 else pair_i, ring(y + s), z, core), columns_used
        )

    for entry in GATHER[at_once:]:
        run(*entry)
    for key in tuple(gathered):
        if key[0] == IMG:
            arrive(*key)

    def arrive_texts(c):
        for key in tuple(gathered):
            _, column, piece, k = key
            base = (piece if column == CORE else column) * 8
            early = ORDER.index(base + ring_slot(k, 0)) >= 8
            if key[0] == TXT and early == (c % 2 == 1) and (column == CORE) == (c >= 2):
                arrive(*key)

    def block(c, sums):
        turn = logits.at[c % 2]
        turn[...] = lax.dot_general(
            txt[pl.ds(c * 256, 256), :], img[...], (((1,), (1,)), ((), ())), preferred_element_type=F32
        )
        tc = core if c < 2 else 1 - core
        pair_sum, slope_sum, scaled_sum = sums
        for k in range(8):
            scaled = turn[tile(k), :] * temp
            u = scaled + shift
            slope, pair = sigmoid_and_softplus(u)
            if (c, k) == (1, 7):
                row = lax.broadcasted_iota(jnp.int32, (T, 512), 0)
                column = lax.broadcasted_iota(jnp.int32, (T, 512), 1)
                own = row + 15 * T == column
                slope = jnp.where(own, 0.0, slope)
                pair = jnp.where(own, 0.0, pair)
            slot = ORDER[c % 2 * 8 + k]
            used = tile_used(pair_t if slot >= 8 else x, y, ring(z + slot), tc)
            weight[pl.ds(c * 256 + k * T, T), :] = (slope * (columns_used[:1] * used * temp)).astype(BF16)

            def folded(value):
                return jnp.sum(value.reshape(T // 8, 8, 512), axis=0)

            pair_sum = pair_sum + used * folded(pair)
            slope_sum = slope_sum + used * folded(slope)
            scaled_sum = scaled_sum + used * folded(slope * scaled)
        return pair_sum, slope_sum, scaled_sum

    def rows_of(group):
        return pl.ds(group * 128, 128)

    def text_dir(first):
        return jnp.dot(weight[first : first + 128, :], img[...], preferred_element_type=F32)

    core_back = {}

    def other_texts(group):
        out_c[rows_of(group), :] = text_dir(512 + group * 128).astype(BF16)
        core_back[group] = fresh()
        send(out_c.at[rows_of(group)], from_c.at[rows_of(group)], core_mate, CORE_BACK, core_back[group])

    zero = jnp.zeros((8, 512), F32)
    totals = (zero, zero, zero)
    for c in range(4):
        arrive_texts(c)
    for c in (3, 2, 1, 0):
        totals = block(c, totals)
        if c == 2:
            other_texts(0)
    pair_sum, slope_sum, scaled_sum = totals

    lane = lax.broadcasted_iota(jnp.int32, (8, 128), 1)

    def own_total():
        whole = [
            jnp.sum(value * columns_used, axis=(0, 1), keepdims=True)
            for value in (pair_sum, slope_sum, scaled_sum)
        ]
        vector = jnp.zeros((8, 128), F32)
        for k in range(3):
            vector = jnp.where(lane == k, whole[k] + own_sums[k], vector)
        return vector

    stage_sems = [fresh() for _ in range(3)]

    def spread(stage, mine, peer_of, value):
        place = scal.at[stage * 8 + mine]
        place[...] = value
        for d in range(1, RING):
            remote(place, place, SCALARS_OUT, stage_sems[stage], peer_of(d)).start()

    def summed(stage):
        others = scal.at[pl.ds(0, RING - 1)]
        remote(others, others, SCALARS_OUT, stage_sems[stage], core_mate).wait_recv()
        total = scal[stage * 8]
        for k in range(1, RING):
            total = total + scal[stage * 8 + k]
        return total

    def own_images(group):
        img_sum[rows_of(group), :] = lax.dot_general(
            weight[:, group * 128 : group * 128 + 128], txt[...], (((0,), (0,)), ((), ())), preferred_element_type=F32
        )

    def own_texts(group):
        txt_sum[rows_of(group), :] = text_dir(group * 128)

    computed = set()

    def compute(ring, group):
        if (ring, group) in computed:
            return
        computed.add((ring, group))
        if ring == IMG:
            own_images(group)
        else:
            own_texts(group)
            if group < 3:
                other_texts(group + 1)

    core_seen = set()

    def own_part(ring, slot, part):
        group = ORDER.index(slot) // 4
        compute(ring, group)
        if ring == IMG:
            return img_sum[at(slot, part), :]
        if group not in core_seen:
            core_seen.add(group)
            wait_for(core_back[group], 128)
        return txt_sum[at(slot, part), :] + from_c[at(slot, part), :].astype(F32)

    out, back = (txt_out, img_out), (txt_back, img_back)
    coming, places = {}, {}

    def landing(column, piece, k, way):
        row = places.setdefault((column, piece, k, way), len(places) * 16)
        return pl.ds(row, 16)

    def received(ring, column, piece, k, way):
        key = (ring, column, piece, k)
        if coming[key] is not None:
            wait_for(*coming[key])
            coming[key] = None
        return back[ring][landing(column, piece, k, way), :].astype(F32)

    def partial(ring, column, piece, k, way):
        value = own_part(ring, column * 8 + ring_slot(k, way), PIECES[piece])
        if column == OWN and ROUTES[piece][MATE][k] is None:
            value = value + received(ring, MATE, piece, k, way)
        for further, parent in ROUTES[piece][column].items():
            if parent != k:
                continue
            if further < 4:
                for w in (0, 1) if k == 0 else (way,):
                    value = value + received(ring, column, piece, further, w)
            else:
                extra = received(ring, column, piece, 4, 0)
                value = value + (extra if k == 0 else jnp.where(odd == way, extra, 0.0))
        return value

    def pass_back(ring, column, piece, k):
        parent, part, index = ROUTES[piece][column][k], PIECES[piece], fresh()
        for way in ways(k):
            slot = column * 8 + ring_slot(k, way)
            out[ring][at(slot, part), :] = partial(ring, column, piece, k, way).astype(BF16)
            if parent is None:
                peer = ring_mate[ring]
            elif k < 4:
                peer = ring_peer[ring]((parent - k) * (1 - 2 * way))
            else:
                peer = ring_peer[ring](jnp.where(odd == 1, k - parent, parent - k))
            target = back[ring].at[landing(column, piece, k, way)]
            send(out[ring].at[at(slot, part)], target, peer, PIECES_BACK, index)
        coming[ring, column, piece, k] = (index, part[1] * len(ways(k)))

    ahead = 0
    for n in range(len(REDUCE) + ahead):
        if n >= ahead:
            pass_back(TXT, *REDUCE[n - ahead])
        if n < len(REDUCE):
            pass_back(IMG, *REDUCE[n])
        if n == 3:
            spread(0, y, y_peer, own_total())
        elif n == 10:
            spread(1, z, z_peer, summed(0))
        elif n == 15:
            spread(2, my_xc, xc_peer, summed(1))

    total = summed(2)
    means = total / used
    scalars[...] = means

    ends = ((txt_unit, txt_length, img_wide, grad_txt), (img_unit, img_length, txt_wide, grad_img))
    for n in (TXT, IMG):
        unit, length, other, grad = ends[n]
        top, low = (partial(n, OWN, piece, 0, 0) for piece in (0, 1))
        total_dir = jnp.concatenate([top, low], axis=0) + own_weight * other
        grad[...] = projected(total_dir, unit, length)

    assert len(used_sems) == N_RECEIVED and len(places) * 16 <= back[0].shape[0]
    for kind, rows in enumerate(rows_sent):
        if rows:
            remote(any_rows(rows), any_rows(rows), kind, 0, core_mate).wait_send()
    scalars_sent = scal.at[pl.ds(0, 3 * (RING - 1))]
    remote(scalars_sent, scalars_sent, SCALARS_OUT, 0, core_mate).wait_send()


def place_results(scalars, grad_img, grad_txt, loss, grad_log_temp, grad_bias, img_out, txt_out, staged, arrived):
    moved = [
        pltpu.make_async_copy(source, target, arrived.at[k])
        for k, (source, target) in enumerate(
            (
                (grad_img, img_out),
                (grad_txt, txt_out),
                (staged.at[0], loss),
                (staged.at[1], grad_bias),
                (staged.at[2], grad_log_temp),
            )
        )
    ]
    for made in moved[:2]:
        made.start()
    for k in range(3):
        staged[k, 0] = scalars[0, k]
        moved[2 + k].start()
    for made in moved:
        made.wait()


def body(images, texts, row_counts, log_temp, bias):
    rows, width = images.shape
    scalar = jax.ShapeDtypeStruct((1,), F32)
    grad = jax.ShapeDtypeStruct((rows, width), F32)
    vmem = pl.BlockSpec(memory_space=pltpu.VMEM)
    found = pl.pallas_call(
        kernel,
        out_shape=(jax.ShapeDtypeStruct((8, 128), F32), grad, grad),
        in_specs=[pl.BlockSpec(memory_space=pltpu.HBM)] * 5,
        out_specs=(vmem, vmem, vmem),
        scratch_shapes=[
            pltpu.VMEM((T, width), BF16),
            pltpu.VMEM((T, width), BF16),
            pltpu.SMEM(row_counts.shape, jnp.int32),
            pltpu.SMEM((1,), F32),
            pltpu.SMEM((1,), F32),
            pltpu.VMEM((512, width), BF16),
            pltpu.VMEM((1024, width), BF16),
            pltpu.VMEM((1024, 512), BF16),
            pltpu.VMEM((2, 256, 512), F32),
            pltpu.VMEM((512, width), BF16),
            pltpu.VMEM((512, width), BF16),
            pltpu.VMEM((512, width), F32),
            pltpu.VMEM((512, width), F32),
            pltpu.VMEM((512, width), BF16),
            pltpu.VMEM((512, width), BF16),
            pltpu.VMEM((480, width), BF16),
            pltpu.VMEM((480, width), BF16),
            pltpu.VMEM((24, 8, 128), F32),
            pltpu.SemaphoreType.DMA((5,)),
            pltpu.SemaphoreType.DMA((N_SENT,)),
            pltpu.SemaphoreType.DMA((N_RECEIVED,)),
        ],
        compiler_params=pltpu.CompilerParams(
            collective_id=0, has_side_effects=True, vmem_limit_bytes=60 << 20
        ),
        cost_estimate=pl.CostEstimate(flops=6 * 512 * 1024 * width, bytes_accessed=4 << 20, transcendentals=1 << 20),
    )(images, texts, row_counts, log_temp, bias)
    return pl.pallas_call(
        place_results,
        out_shape=(scalar, scalar, scalar, grad, grad),
        in_specs=[vmem] * 3,
        out_specs=[pl.BlockSpec(memory_space=pltpu.HBM)] * 5,
        scratch_shapes=[pltpu.SMEM((3, 1), F32), pltpu.SemaphoreType.DMA((5,))],
    )(*found)


def solution(mesh):
    return jax.shard_map(
        body,
        mesh=mesh,
        in_specs=(P(("blk", "sub"), None), P(("blk", "sub"), None), P(), P(), P()),
        out_specs=(P(), P(), P(), P(("blk", "sub"), None), P(("blk", "sub"), None)),
        check_vma=False,
    )
```
